256 devices in a mesh: expert: 8 (over x, core), tensor: 32 (over y, z).
Axes of the slice: x: 4, y: 4, z: 8, core: 2. Of those that a mesh axis runs over, the one named last changes fastest.
Arguments:
- tokens: bfloat16 [1024, 6144], P('expert'), may hold values from -6 to 6
- routes: int32 [1024, 2], P('expert'), may hold values from 0 to 7, all different within a row; in each aligned block of 128 rows (0 to 127, 128 to 255, ...) at most 64 rows name the same one
- gate_num: int32 [1024, 2], P('expert'), may hold values from 1 to 15
- gate_weight: bfloat16 [8, 6144, 8192], P('expert', None, 'tensor'), may hold values from -0.078125 to 0.078125
- up_weight: bfloat16 [8, 6144, 8192], P('expert', None, 'tensor'), may hold values from -0.078125 to 0.078125
- down_weight: bfloat16 [8, 8192, 6144], P('expert', 'tensor'), may hold values from -0.125 to 0.125
Outputs:
- mixed: bfloat16 [1024, 6144], P('expert', 'tensor')
The draws below stay inside these ranges and needn't reach their ends.
Inputs may be any that keep to these rules, and one draw needn't show every extreme that they name: `routes`: within the 128 tokens of one index of expert, the two experts of a token differ, no expert is named by more than 64 tokens, a bound that some block reaches.
All inputs are finite; a program needn't handle non-finite values.
Results may differ from the reference program's by a relative error of at most 0.027.
Values may be sent and summed in bfloat16 or wider, within the bound.
A program may use at most 64 MiB of HBM per device.

```python
import math
import jax
import jax.numpy as jnp
import numpy as np
from jax import lax

D = 6144
FF = 8192
TOK_DEV = 128
CAP = 64
EXPERTS = 8
TOKENS = 1024
N_EXPERT = 8
N_TENSOR = 32


def touch_ends(values, rng, smallest, high):
    spot = [jax.random.randint(jax.random.fold_in(rng, axis), (), 0, length) for axis, length in enumerate(values.shape)]
    widest = values.shape.index(max(values.shape))
    next_to = spot[:widest] + [(spot[widest] + 1) % values.shape[widest]] + spot[widest + 1:]
    return values.at[tuple(spot)].set(smallest).at[tuple(next_to)].set(high)


def with_spikes(drawn, own_key, source, target, shards_of, factor):
    owner, partner = [(jnp.arange(drawn.shape[axis_at]) // (drawn.shape[axis_at] // shards_of)).reshape([-1 if axis == axis_at else 1 for axis in range(drawn.ndim)]) for axis_at in (source, target)]
    chosen = jax.random.permutation(own_key, shards_of)[partner]
    strong = (owner == chosen) | (owner == (partner + shards_of // 2) % shards_of)
    return jnp.where(strong, factor * drawn, drawn)


def levels(stream_key, extent, split, smallest, largest):
    factor_of, own = 1.0, jax.random.fold_in(stream_key, 6)
    for axis_at, shards_of in split:
        heights = jnp.exp(jax.random.uniform(jax.random.fold_in(own, axis_at), (shards_of,), jnp.float32, smallest / len(split), largest / len(split)))
        factor_of = factor_of * jnp.repeat(heights, extent[axis_at] // shards_of).reshape([-1 if axis == axis_at else 1 for axis in range(len(extent))])
    return factor_of


def assign_block(key, own, number, rows, amount, top, most, lean):
    ranking = jax.random.permutation(key, amount)
    heavy_load, ordinary = portions_of(amount, rows * top, most, lean, True), portions_of(amount, rows * top, most, lean, False)
    places = jnp.arange(amount)

    def named(tallies, turn):
        used = int((tallies > 0).sum())
        fixed = max(1, used // 4)
        moved = fixed + (places - fixed + turn * (used - fixed)) % max(1, amount - fixed)
        return jnp.zeros((amount,), jnp.int32).at[ranking[jnp.where(places < fixed, places, moved)]].set(jnp.asarray(tallies, jnp.int32))

    tallies = jnp.where(number % 4 == 0, named(heavy_load, number // 4), named(ordinary, number - number // 4 - 1))
    mixed = jax.random.permutation(jax.random.fold_in(own, 3), amount)
    donor, taker = mixed[0:amount // 2 * 2:2], mixed[1:amount // 2 * 2:2]
    margin = jnp.minimum(tallies[donor] - 1, most - tallies[taker]) // 2
    margin = jnp.where((donor == ranking[0]) | (taker == ranking[0]) | (tallies[taker] == 0), 0, jnp.maximum(margin, 0))
    moved = jax.random.randint(jax.random.fold_in(own, 4), (amount // 2,), 0, 1 << 20) % (margin + 1)
    tallies = tallies.at[donor].add(-moved).at[taker].add(moved)
    items = jnp.searchsorted(jnp.cumsum(tallies), jnp.arange(rows * top), side="right").astype(jnp.int32)
    grid = items.reshape(top, rows).T
    grid = grid[jax.random.permutation(jax.random.fold_in(own, 1), rows)]
    turn = jax.random.randint(jax.random.fold_in(own, 2), (rows, 1), 0, top)
    return jnp.take_along_axis(grid, (jnp.arange(top)[None, :] + turn) % top, axis=1)


def portions_of(count, total, limit, lean, full):
    portions = [(1 << 20) // math.isqrt(rank ** lean) + 1 for rank in range(1, count + 1)]
    largest = limit if full else min(limit, max(-(-total // count), total * portions[0] // sum(portions)))
    least = 1 if total - largest >= count - 1 else 0
    counts, rest = [largest] + [least] * (count - 1), total - largest - least * (count - 1)
    while rest > 0:
        free = [i for i in range(1, count) if counts[i] < largest] or [i for i in range(1, count) if counts[i] < limit]
        mass, left = sum([portions[i] for i in free]), rest
        for i in free:
            more = min(limit - counts[i], max(1, left * portions[i] // mass), rest)
            counts[i] = counts[i] + more
            rest = rest - more
    return np.array(counts)


def noise(stream_key, extent, spread, limit, shards=(), held_as=jnp.bfloat16):
    values = spread * jax.random.normal(stream_key, extent, jnp.float32)
    if shards:
        values = values * levels(stream_key, extent, shards, -0.22, 0.18)
    return jnp.clip(values, -limit, limit).astype(held_as)


def gaussian_with(own_key, extent, deviation, bound, cuts, heavy, kind=jnp.bfloat16):
    values = deviation * jax.random.normal(own_key, extent, jnp.float32)
    if cuts:
        values = values * levels(own_key, extent, cuts, -0.22, 0.18)
    return jnp.clip(with_spikes(values, jax.random.fold_in(own_key, 3), *heavy), -bound, bound).astype(kind)


def setup_inputs(seed: int = 0) -> dict:
    streams_of = jax.random.split(jax.random.key(seed), 7)
    tokens = noise(streams_of[0], (TOKENS, D), 1.0, 6.0, ((0, 8),))
    routes_keys = jax.random.split(jax.random.fold_in(streams_of[1], 1), TOKENS // TOK_DEV)
    routes_turns = jax.random.permutation(jax.random.fold_in(streams_of[1], 3), TOKENS // TOK_DEV)
    routes = jax.vmap(lambda own, number: assign_block(jax.random.fold_in(streams_of[1], 2), own, number, TOK_DEV, EXPERTS, 2, CAP, 2))(routes_keys, routes_turns).reshape((TOKENS, 2))
    gate_num = touch_ends(jax.random.randint(streams_of[2], (TOKENS, 2), 1, 16), jax.random.fold_in(streams_of[2], 1), 1, 15).astype(jnp.int32)
    gate_weight = noise(streams_of[3], (EXPERTS, D, FF), D ** -0.5, 0.078125, ((0, 8), (2, 32)))
    up_weight = noise(streams_of[4], (EXPERTS, D, FF), D ** -0.5, 0.078125, ((0, 8), (2, 32)))
    down_weight = gaussian_with(streams_of[5], (EXPERTS, FF, D), FF ** -0.5, 0.125, ((0, 8), (1, 32)), (1, 2, 32, 2.75))
    return dict(tokens=tokens, routes=routes, gate_num=gate_num, gate_weight=gate_weight, up_weight=up_weight, down_weight=down_weight)


denominator = 16.0

def slot_tables(route_block, numer_block, expert_count):
    chosen = route_block.reshape(-1).astype(jnp.int32)
    expert_row = jnp.arange(expert_count, dtype=jnp.int32)
    onehot = (chosen[:, None] == expert_row[None, :]).astype(jnp.int32)
    before = jnp.cumsum(onehot, axis=0) - onehot
    slot_index = lax.optimization_barrier(jnp.sum(before * onehot, axis=1))
    target_slot = chosen * CAP + slot_index
    targets = jnp.arange(expert_count * CAP, dtype=jnp.int32)
    matches = (target_slot[None, :] == targets[:, None]).astype(jnp.float32)
    matches = matches.reshape(expert_count * CAP, -1, 2)
    dispatch = lax.optimization_barrier(jnp.sum(matches, axis=2))
    weights = numer_block.astype(jnp.float32) / denominator
    combine = lax.optimization_barrier(jnp.sum(matches * weights[None, :, :], axis=2)).T
    return (dispatch, combine)

def walsh(values):
    row_total = values.shape[0]
    length = values.shape[1]
    for step_number in range(length.bit_length() - 1):
        stride = 2 ** step_number
        shaped = values.reshape(row_total, length // (2 * stride), 2, stride)
        first = shaped[:, :, 0]
        second = shaped[:, :, 1]
        values = jnp.stack([first + second, first - second], axis=2).reshape(row_total, length)
    return values

def reference(tokens, routes, gate_num, gate_weight, up_weight, down_weight):
    local_hidden = FF // N_TENSOR
    token_blocks = tokens.reshape(N_EXPERT, TOK_DEV, D)
    route_blocks = routes.reshape(N_EXPERT, TOK_DEV, 2)
    numer_blocks = gate_num.reshape(N_EXPERT, TOK_DEV, 2)
    outgoing_all = []
    combine_all = []
    for block_number in range(N_EXPERT):
        dispatch, combine = slot_tables(route_blocks[block_number], numer_blocks[block_number], EXPERTS)
        outgoing = jnp.dot(dispatch.astype(jnp.bfloat16), token_blocks[block_number], preferred_element_type=jnp.float32)
        outgoing_all.append(outgoing.astype(jnp.bfloat16).reshape(EXPERTS, CAP, D))
        combine_all.append(combine)
    outgoing_all = jnp.stack(outgoing_all, axis=0)
    expert_outs = []
    for expert_number in range(EXPERTS):
        expert_rows = outgoing_all[:, expert_number].reshape(N_EXPERT * CAP, D)
        gate_value = jnp.dot(expert_rows, gate_weight[expert_number], preferred_element_type=jnp.float32)
        up_value = jnp.dot(expert_rows, up_weight[expert_number], preferred_element_type=jnp.float32)
        hidden = (jax.nn.silu(gate_value) * up_value).astype(jnp.bfloat16)
        rotated = (walsh(hidden.astype(jnp.float32)) * (1.0 / math.sqrt(FF))).astype(jnp.bfloat16)
        running_sum = jnp.zeros((N_EXPERT * CAP, D), jnp.float32)
        for part_number in range(N_TENSOR):
            lower = part_number * local_hidden
            piece = jnp.dot(rotated[:, lower:lower + local_hidden], down_weight[expert_number, lower:lower + local_hidden], preferred_element_type=jnp.float32)
            rounded = lax.optimization_barrier(piece.astype(jnp.bfloat16))
            running_sum = running_sum + rounded.astype(jnp.float32)
        expert_outs.append(running_sum.reshape(N_EXPERT, CAP, D))
    expert_outs = jnp.stack(expert_outs, axis=1)
    results = []
    for block_number in range(N_EXPERT):
        slot_rows = expert_outs[block_number].reshape(EXPERTS * CAP, D)
        token_rows = jnp.dot(combine_all[block_number], slot_rows, preferred_element_type=jnp.float32, precision=lax.Precision.HIGHEST)
        results.append(token_rows.astype(jnp.bfloat16))
    return jnp.concatenate(results, axis=0)
```

```python
import math

import jax
import jax.numpy as jnp
from jax import lax
from jax.experimental import pallas as pl
from jax.experimental.pallas import tpu as pltpu
from jax.sharding import PartitionSpec as P

NX, NY, NZ, NT = 4, 4, 8, 32
CAP, TOK, D, HID = 64, 128, 6144, 256
YZ_COLS = NT * 128
MESH = pl.DeviceIdType.MESH
BF16, F32 = jnp.bfloat16, jnp.float32

GATHER_P, GATHER_Q = (128, 224), (352, 160)
REDUCE_P, REDUCE_Q = (0, 288), (288, 224)


class Node:
    def __init__(self, deps, cost, act=None, way=None, size=0, src=None, dst=None):
        self.deps, self.cost, self.act = list(deps), cost, act
        self.way, self.size, self.src, self.dst = way, size, src, dst


def steps_of(nodes):
    done, sent, steps, now, link, due = set(), set(), [], 0.0, {}, {}

    def send_ready():
        for i, node in enumerate(nodes):
            if node.way and i not in sent and all(d in done for d in node.deps):
                begin = max(now, link.get(node.way, 0.0))
                link[node.way] = begin + node.size * 2 / 1e5
                due[i] = link[node.way] + 1.6
                sent.add(i)
                steps.append(("send", i))

    send_ready()
    while len(done) < len(nodes):
        coming = sorted((due[i], i) for i in sent - done)
        tasks = [i for i, n in enumerate(nodes) if not n.way and i not in done and all(d in done for d in n.deps)]
        if coming and coming[0][0] <= now:
            pick = coming[0][1]
        elif tasks:
            pick = tasks[0]
        else:
            now, pick = coming[0]
        steps.append(("take" if nodes[pick].way else "task", pick))
        done.add(pick)
        now += nodes[pick].cost
        send_ready()
    return steps


def halves(rows):
    low, count = rows
    return (low, count // 2), (low + count // 2, count // 2)


def tree(p_rows, q_rows):
    found = []

    def add(way, slot, rows, deps):
        found.append((way, slot, rows, list(deps)))
        return len(found) - 1

    def ring(offset_y, rows, deps, arrived):
        for way, half in ((1, 0), (-1, 1)):
            before = deps
            for step in range(4):
                part = rows if step < 3 else halves(rows)[half]
                before = [add((0, way), (offset_y, -way * step), part, before)]
                arrived.setdefault(way * 4 if step == 3 else -way * (step + 1), []).extend(before)

    arrived = {}
    ring(0, p_rows, [], arrived)
    arrived = {0: [], 4: arrived.pop(4) + arrived.pop(-4), **arrived}
    for offset_z in (4, 3, -3, 2, -2, 1, -1, 0):
        up = add((1, 0), (0, offset_z), p_rows, arrived[offset_z])
        down = add((-1, 0), (0, offset_z), p_rows, arrived[offset_z])
        add((1, 0), (-1, offset_z), halves(p_rows)[0], [up])
        add((-1, 0), (1, offset_z), halves(p_rows)[1], [down])
    up = add((1, 0), (0, 0), q_rows, [])
    down = add((-1, 0), (0, 0), q_rows, [])
    far = [add((1, 0), (-1, 0), halves(q_rows)[0], [up]), add((-1, 0), (1, 0), halves(q_rows)[1], [down])]
    for offset_y, deps in ((0, []), (-1, [up]), (1, [down]), (2, far)):
        ring(offset_y, q_rows, deps, {})
    return found


def kernel(
    meta_ref, tok_ref, gate_ref, up_ref, down_ref, main_ref, extra_ref,
    metas, weights, downs, tiles, wide, acc, pick, blend, fold, mix, sent_rows, got_rows, back_rows, turned, mixed_in,
    part, part_in, cross, cross_in, over, over_in, last_in,
    a_send, a_recv, b_send, b_recv, c_send, c_recv, w_send, w_recv, w_own,
):
    own_e, own_t = lax.axis_index("expert"), lax.axis_index("tensor")
    x, c = lax.div(own_e, 2), lax.rem(own_e, 2)
    y, z = lax.div(own_t, NZ), lax.rem(own_t, NZ)

    def slot(dy, dz):
        return lax.rem(y + dy + NY, NY) * NZ + lax.rem(z + dz + NZ, NZ)

    def device(dx, dy, dz):
        return (lax.rem(x + dx + NX, NX) * 2 + c, slot(dy, dz))

    sibling = (x * 2 + 1 - c, own_t)

    barrier = pltpu.get_barrier_semaphore()
    for dx in (1, 2, 3):
        pl.semaphore_signal(barrier, inc=1, device_id=device(dx, 0, 0), device_id_type=MESH)
    pl.semaphore_signal(barrier, inc=1, device_id=sibling, device_id_type=MESH)

    def greet(k, carry):
        pl.semaphore_signal(barrier, inc=1, device_id=device(0, lax.div(k, NZ), lax.rem(k, NZ)), device_id_type=MESH)
        return carry

    lax.fori_loop(1, NT, greet, 0)

    def weight_part(number):
        group, which = number // 2, number % 2
        low = lax.rem(y + group, NY) * 1024 if group < 4 else 1024 * group
        return (gate_ref, up_ref)[which].at[pl.ds(low, 1024)], lambda expert: weights.at[expert, which, pl.ds(low, 1024)]

    def own_copy(number):
        if number < 12:
            src, dst = weight_part(number)
            return pltpu.make_async_copy(src, dst(0), w_own.at[number])
        return pltpu.make_async_copy(down_ref, downs.at[pl.ds(0, HID)], w_own.at[number])

    def sibling_copy(number):
        if number < 12:
            src, dst = weight_part(number)
            dst = dst(1)
        else:
            src, dst = down_ref, downs.at[pl.ds(HID, HID)]
        return pltpu.make_async_remote_copy(
            src_ref=src, dst_ref=dst, send_sem=w_send.at[number], recv_sem=w_recv.at[number],
            device_id=sibling, device_id_type=MESH,
        )

    for number in range(13):
        own_copy(number).start()

    def copy_of(node, number, send, recv):
        return pltpu.make_async_remote_copy(
            src_ref=node.src(), dst_ref=node.dst(), send_sem=send.at[number], recv_sem=recv.at[number],
            device_id=device(*node.way), device_id_type=MESH,
        )

    def run(nodes, send, recv):
        for kind, i in steps_of(nodes):
            if kind == "send":
                copy_of(nodes[i], i, send, recv).start()
            else:
                if kind == "take":
                    copy_of(nodes[i], i, send, recv).wait_recv()
                if nodes[i].act:
                    nodes[i].act()

    def finish(nodes, send, recv):
        for i, node in enumerate(nodes):
            if node.way:
                copy_of(node, i, send, recv).wait_send()

    nodes_a = []

    def message(nodes, way, size, src, dst, deps=(), act=None, cost=0.05):
        nodes.append(Node(deps, cost, act, way, size, src, dst))
        return len(nodes) - 1

    def task(nodes, act, deps, cost):
        nodes.append(Node(deps, cost, act))
        return len(nodes) - 1

    slices, meta_nodes = [], []
    for dx in (1, -1, 2):
        slices.append(message(
            nodes_a, (dx, 0, 0), 32768,
            lambda: tok_ref.at[:, pl.ds(pl.multiple_of(own_t * 128, 128), 128)],
            lambda dx=dx: tiles.at[own_t, pl.ds((-dx) % 4 * TOK, TOK)],
        ))
    for dx in (1, -1, 2):
        meta_nodes.append(message(
            nodes_a, (dx, 0, 0), 4096, lambda: meta_ref, lambda dx=dx: metas.at[(-dx) % 4],
        ))
    chunk_nodes = []
    for k in range(4):
        found = []
        for dx in (1, -1):
            found.append(message(
                nodes_a, (dx, 0, 0), 131072,
                lambda k=k: tok_ref.at[:, pl.ds(YZ_COLS + 512 * k, 512)],
                lambda k=k, dx=dx: wide.at[k, pl.ds((-dx) % 4 * TOK, TOK)],
            ))
        chunk_nodes.append(found)
    for k in range(4):
        dx = 1 if k < 2 else -1
        chunk_nodes[k].append(message(
            nodes_a, (dx, 0, 0), 131072,
            lambda k=k, dx=dx: wide.at[k, pl.ds((-dx) % 4 * TOK, TOK)],
            lambda k=k: wide.at[k, pl.ds(2 * TOK, TOK)],
            [chunk_nodes[k][0 if k < 2 else 1]],
        ))
    gather = tree(GATHER_P, GATHER_Q)
    base = len(nodes_a)
    group_nodes = [list(slices), [], [], []]
    for (dy, dz), (sy, sz), (low, count), deps in gather:
        def ref(sy=sy, sz=sz, low=low, count=count):
            return tiles.at[slot(sy, sz), pl.ds(low, count)]

        number = message(nodes_a, (0, dy, dz), count * 256, ref, ref, [base + d for d in deps] if deps else slices)
        group_nodes[(sy - dy) % 4].append(number)

    def expert_id(i):
        return 2 * x + (c if i == 0 else 1 - c)

    def fill():
        metas[0] = meta_ref[...]
        for number in range(13):
            sibling_copy(number).start()
        for t in range(NT):
            tiles[t, 0:TOK, :] = tok_ref[:, t * 128 : (t + 1) * 128]
        for k in range(4):
            wide[k, 0:TOK, :] = tok_ref[:, YZ_COLS + 512 * k : YZ_COLS + 512 * (k + 1)]

    def signs():
        def sign(row, column):
            common = row & column
            common = common ^ (common >> 4)
            common = common ^ (common >> 2)
            common = common ^ (common >> 1)
            return (1 - 2 * (common & 1)).astype(F32)

        def both(order):
            return lax.broadcasted_iota(jnp.int32, (order, order), 0), lax.broadcasted_iota(jnp.int32, (order, order), 1)

        row, column = both(HID)
        fold[...] = sign(row, column).astype(BF16)
        row, column = both(2 * HID)
        same = (row & 15) == (column & 15)
        mix[...] = jnp.where(same, sign(row >> 4, column >> 4), 0.0).astype(BF16)

    def tables():
        earlier = lax.broadcasted_iota(jnp.int32, (TOK, TOK), 0) < lax.broadcasted_iota(jnp.int32, (TOK, TOK), 1)
        earlier = earlier.astype(F32).astype(BF16)
        slots = lax.broadcasted_iota(jnp.int32, (CAP, TOK), 0).astype(F32)
        for dx in range(NX):
            first, second = metas[dx, 0:1, :], metas[dx, 1:2, :]
            gain_1, gain_2 = metas[dx, 2:3, :].astype(F32), metas[dx, 3:4, :].astype(F32)
            for i in range(2):
                is_1 = (first == expert_id(i)).astype(F32)
                is_2 = (second == expert_id(i)).astype(F32)
                named = is_1 + is_2
                place = jnp.dot(
                    jnp.broadcast_to(named, (16, TOK)).astype(BF16), earlier, preferred_element_type=F32
                )[0:1]
                hit = jnp.where(slots == place, 1.0, 0.0) * named
                pick[i, dx] = hit.astype(BF16)
                blend[i, dx] = (hit * ((is_1 * gain_1 + is_2 * gain_2) * (1.0 / 16.0))).astype(BF16)

    def weights_wait(group):
        for number in (2 * group, 2 * group + 1):
            own_copy(number).wait()
            sibling_copy(number).wait_recv()

    started = []

    def accumulate(rows, low, count):
        fresh = not started
        started.append(low)
        for i in range(2):
            for which in range(2):
                term = jnp.dot(rows, weights[i, which, pl.ds(low, count), :], preferred_element_type=F32)
                acc[i, which] = term if fresh else acc[i, which] + term

    def group_dot(group):
        weights_wait(group)
        base_y = lax.rem(y + group, NY)
        rows = jnp.concatenate([tiles[base_y * NZ + j] for j in range(NZ)], axis=1)
        accumulate(rows, base_y * 1024, 1024)

    def chunk_dot(k):
        if k % 2 == 0:
            weights_wait(4 + k // 2)
        accumulate(wide[k], YZ_COLS + 512 * k, 512)

    fill_task = task(nodes_a, fill, [], 0.6)
    sign_task = task(nodes_a, signs, [], 1.0)
    task(nodes_a, tables, meta_nodes + [fill_task], 0.6)
    last = sign_task
    for k in range(4):
        last = task(nodes_a, lambda k=k: chunk_dot(k), chunk_nodes[k] + [last], 0.6)
    for group in (0, 1, 3, 2):
        task(nodes_a, lambda group=group: group_dot(group), group_nodes[group] + [sign_task], 1.0)

    pl.semaphore_wait(barrier, NT - 1 + 4)
    run(nodes_a, a_send, a_recv)

    for i in range(2):
        gate, up = acc[i, 0], acc[i, 1]
        turned[...] = (gate / (1.0 + jnp.exp(-gate)) * up).astype(BF16)
        for dx in range(NX):
            chosen = jnp.dot(pick[i, dx], turned[dx * TOK : (dx + 1) * TOK, :], preferred_element_type=F32).astype(BF16)
            low = (i * NX + dx) * CAP
            sent_rows[low : low + CAP, :] = jnp.dot(chosen, fold[...], preferred_element_type=F32).astype(BF16)

    def piece(ref, t):
        return ref.at[pl.ds(pl.multiple_of(t * 16, 16), 16)]

    def exchange(src, dst, first):
        def copy(k):
            other = slot(lax.div(k, NZ), lax.rem(k, NZ))
            return pltpu.make_async_remote_copy(
                src_ref=piece(src, other), dst_ref=piece(dst, own_t),
                send_sem=b_send.at[first + k], recv_sem=b_recv.at[first + k],
                device_id=(own_e, other), device_id_type=MESH,
            )

        lax.fori_loop(1, NT, lambda k, u: (copy(k).start(), u)[1], 0)
        keep = pl.ds(pl.multiple_of(own_t * 16, 16), 16)
        dst[keep, :] = src[keep, :]
        lax.fori_loop(1, NT, lambda k, u: (copy(k).wait_recv(), u)[1], 0)
        return lambda: lax.fori_loop(1, NT, lambda k, u: (copy(k).wait_send(), u)[1], 0)

    sends_1 = exchange(sent_rows, got_rows, 0)
    values = jnp.dot(mix[...], got_rows[...], preferred_element_type=F32)
    back_rows[...] = (values * (1.0 / math.sqrt(NT * HID))).astype(BF16)
    sends_2 = exchange(back_rows, turned, NT)

    for i in range(2):
        for dx in range(NX):
            low = (i * NX + dx) * CAP
            spread = lax.dot_general(
                blend[i, dx], turned[low : low + CAP, :], (((0,), (0,)), ((), ())), preferred_element_type=F32
            )
            mixed_in[dx * TOK : (dx + 1) * TOK, i * HID : (i + 1) * HID] = spread.astype(BF16)
    own_copy(12).wait()
    sibling_copy(12).wait_recv()

    nodes_c = []

    def down_dot(group):
        base_y = lax.rem(y + group, NY)
        for half in range(2):
            columns = pl.ds(pl.multiple_of(base_y * 1536 + half * 768, 128), 768)
            values = jnp.dot(mixed_in[...], downs[:, columns], preferred_element_type=F32).astype(BF16)
            for pair in range(2):
                q = 2 * half + pair
                low = 384 * pair
                part[base_y * NZ + 2 * q] = values[:, low : low + 128]
                part[base_y * NZ + 2 * q + 1] = values[:, low + 256 : low + 384]
                for dx in range(NX):
                    cross[group, dx, q] = values[dx * TOK : (dx + 1) * TOK, low + 128 : low + 256]

    group_task = {}
    for group in (2, 1, 3, 0):
        group_task[group] = task(nodes_c, lambda group=group: down_dot(group), [], 1.0)

    base = len(nodes_c)
    reduction = tree(REDUCE_P, REDUCE_Q)
    total = 0
    roots = [group_task[0]]
    for number, ((dy, dz), (sy, sz), (low, count), deps) in enumerate(reduction):
        def src(sy=sy, sz=sz, dy=dy, dz=dz, low=low, count=count):
            return part.at[slot(sy - dy, sz - dz), pl.ds(low, count)]

        def dst(total=total, count=count):
            return part_in.at[pl.ds(total, count)]

        def act(sy=sy, sz=sz, low=low, count=count, total=total):
            here = slot(sy, sz)
            part[here, low : low + count, :] = part[here, low : low + count, :] + part_in[total : total + count, :]

        children = [base + n for n, other in enumerate(reduction) if number in other[3]]
        if not deps:
            roots.append(base + number)
        message(
            nodes_c, (0, -dy, -dz), count * 256, src, dst, children + [group_task[(sy - dy) % 4]], act, 0.1
        )
        total += count

    packed = {}
    for group in (2, 1, 3, 0):
        def add_cross(dx, low, count, index, group=group):
            for q in range(low, low + count):
                cross[group, dx, q] = cross[group, dx, q] + cross_in[group, index, q]

        def hop(way, dx, low, count, index, into, deps, group=group, add_cross=add_cross):
            return message(
                nodes_c, (way, 0, 0), count * 32768,
                lambda: cross.at[group, dx, pl.ds(low, count)],
                lambda: cross_in.at[group, index, pl.ds(low, count)],
                deps, lambda: add_cross(into, low, count, index), 0.2,
            )

        ready = group_task[group]
        far_1 = hop(-1, 2, 0, 2, 0, 3, [ready])
        far_2 = hop(1, 2, 2, 2, 0, 1, [ready])
        near_1 = hop(-1, 3, 0, 4, 1, 0, [ready, far_1])
        near_2 = hop(1, 1, 0, 4, 2, 0, [ready, far_2])

        def pack(group=group):
            lane = lax.broadcasted_iota(jnp.int32, (CAP, 128), 1)
            for q in range(4):
                top, low = cross[group, 0, q, 0:CAP, :].astype(F32), cross[group, 0, q, CAP:TOK, :].astype(F32)
                over[group, 2 * q] = jnp.where(lane < 64, top, pltpu.roll(low, 64, 1)).astype(BF16)
                over[group, 2 * q + 1] = jnp.where(lane < 64, pltpu.roll(top, 64, 1), low).astype(BF16)

        packed[group] = task(nodes_c, pack, [near_1, near_2, ready], 0.3)

    def add_over(group, low, count, index):
        for n in range(low, low + count):
            over[group, n] = over[group, n] + over_in[index, n]

    def over_hop(way, group, low, count, index, into, deps):
        return message(
            nodes_c, (0, way, 0), count * 16384,
            lambda: over.at[group, pl.ds(low, count)], lambda: over_in.at[index, pl.ds(low, count)],
            deps, lambda: add_over(into, low, count, index), 0.1,
        )

    far_1 = over_hop(-1, 2, 0, 4, 0, 3, [packed[2]])
    far_2 = over_hop(1, 2, 4, 4, 0, 1, [packed[2]])
    near_1 = over_hop(-1, 3, 0, 8, 1, 0, [packed[3], far_1])
    near_2 = over_hop(1, 1, 0, 8, 2, 0, [packed[1], far_2])
    ends = []
    for way, low, index in ((1, 0, 3), (-1, 32, 4)):
        before = [near_1, near_2, packed[0]]
        for step in (3, 2, 1, 0):
            rows = pl.ds(low, 32) if step == 3 else pl.ds(0, CAP)

            def src(way=way, step=step, rows=rows):
                return over.at[0, lax.rem(z - way * (step + 1) + NZ, NZ), rows]

            def dst(step=step, rows=rows, index=index):
                return over_in.at[index, step, rows]

            def act(way=way, step=step, rows=rows, index=index):
                here = lax.rem(z - way * step + NZ, NZ)
                over[0, here, rows, :] = over[0, here, rows, :] + over_in[index, step, rows, :]

            size = (32 if step == 3 else CAP) * 256
            before = [near_1, near_2, packed[0], message(nodes_c, (0, 0, -way), size, src, dst, before, act, 0.05)]
        ends.append(before[-1])

    lasts = []
    for dx in (2, 1, -1):
        lasts.append(message(
            nodes_c, (dx, 0, 0), 32768, lambda dx=dx: part.at[own_t, pl.ds(dx % 4 * TOK, TOK)],
            lambda dx=dx: last_in.at[(-dx) % 4], roots,
        ))

    def store():
        summed = part[own_t, 0:TOK, :].astype(F32)
        for dx in (1, 2, 3):
            summed = summed + last_in[dx].astype(F32)
        main_ref[...] = summed.astype(BF16)
        extra_ref[...] = over[0, z]

    task(nodes_c, store, lasts + ends, 0.2)
    run(nodes_c, c_send, c_recv)

    finish(nodes_a, a_send, a_recv)
    for number in range(13):
        sibling_copy(number).wait_send()
    sends_1()
    sends_2()
    finish(nodes_c, c_send, c_recv)


def shards(tokens, routes, gate_num, gate_weight, up_weight, down_weight):
    meta = jnp.concatenate([routes.T, gate_num.T, jnp.zeros((4, TOK), jnp.int32)], axis=0)
    vmem, anywhere = pl.BlockSpec(memory_space=pltpu.VMEM), pl.BlockSpec(memory_space=pl.ANY)
    dma = pltpu.SemaphoreType.DMA
    main, extra = pl.pallas_call(
        kernel,
        out_shape=(jax.ShapeDtypeStruct((TOK, 128), BF16), jax.ShapeDtypeStruct((CAP, 128), BF16)),
        in_specs=[vmem, vmem, anywhere, anywhere, anywhere],
        out_specs=(vmem, vmem),
        scratch_shapes=[
            pltpu.VMEM((NX, 8, TOK), jnp.int32),
            pltpu.VMEM((2, 2, D, HID), BF16),
            pltpu.VMEM((2 * HID, D), BF16),
            pltpu.VMEM((NT, NX * TOK, 128), BF16),
            pltpu.VMEM((4, NX * TOK, 512), BF16),
            pltpu.VMEM((2, 2, NX * TOK, HID), F32),
            pltpu.VMEM((2, NX, CAP, TOK), BF16),
            pltpu.VMEM((2, NX, CAP, TOK), BF16),
            pltpu.VMEM((HID, HID), BF16),
            pltpu.VMEM((2 * HID, 2 * HID), BF16),
            pltpu.VMEM((2 * NX * CAP, HID), BF16),
            pltpu.VMEM((2 * NX * CAP, HID), BF16),
            pltpu.VMEM((2 * NX * CAP, HID), BF16),
            pltpu.VMEM((2 * NX * CAP, HID), BF16),
            pltpu.VMEM((NX * TOK, 2 * HID), BF16),
            pltpu.VMEM((NT, NX * TOK, 128), BF16),
            pltpu.VMEM((15872, 128), BF16),
            pltpu.VMEM((4, NX, 4, TOK, 128), BF16),
            pltpu.VMEM((4, 3, 4, TOK, 128), BF16),
            pltpu.VMEM((4, NZ, CAP, 128), BF16),
            pltpu.VMEM((5, NZ, CAP, 128), BF16),
            pltpu.VMEM((NX, TOK, 128), BF16),
            dma((100,)), dma((100,)), dma((64,)), dma((64,)), dma((128,)), dma((128,)),
            dma((13,)), dma((13,)), dma((13,)),
        ],
        compiler_params=pltpu.CompilerParams(
            collective_id=0, has_side_effects=True, vmem_limit_bytes=60 * 2**20
        ),
        cost_estimate=pl.CostEstimate(flops=10**10, bytes_accessed=2 * 10**7, transcendentals=2**18),
        name="moe_layer",
    )(meta, tokens, gate_weight[0], up_weight[0], down_weight[0])
    extra = jnp.concatenate([extra[:, :64], extra[:, 64:]], axis=0)
    odd = lax.rem(lax.axis_index("tensor"), 2) == 1
    return jnp.where(odd, jnp.concatenate([extra, main], axis=1), jnp.concatenate([main, extra], axis=1))


def solution(mesh):
    placed = (
        P("expert", None),
        P("expert", None),
        P("expert", None),
        P("expert", None, "tensor"),
        P("expert", None, "tensor"),
        P("expert", "tensor", None),
    )
    return jax.shard_map(
        shards, mesh=mesh, in_specs=placed, out_specs=P("expert", "tensor"), check_vma=False
    )
```

```python
import math

import jax
import jax.numpy as jnp
from jax import lax
from jax.experimental import pallas as pl
from jax.experimental.pallas import tpu as pltpu
from jax.sharding import PartitionSpec as P

NX, NY, NZ, NT = 4, 4, 8, 32
CAP, TOK, D, HID = 64, 128, 6144, 256
YZ_COLS = NT * 128
MESH = pl.DeviceIdType.MESH
BF16, F32 = jnp.bfloat16, jnp.float32

PEERS = tuple((dx, dc) for dx in (0, 2, 1, 3) for dc in (0, 1))
GATHER = ((128, 224), (352, 160))
REDUCE = ((0, 288), (288, 224))
LATENCY, B_PAUSE = 2.2, 6.0


class Node:
    def __init__(self, deps, cost, act=None, way=None, size=0, src=None, dst=None, pause=0.0, bundle=None, sender=None):
        self.deps, self.cost, self.act, self.pause = list(deps), cost, act, pause
        self.way, self.size, self.src, self.dst, self.bundle, self.sender = way, size, src, dst, bundle, sender


def steps_of(nodes):
    done, sent, steps, now, link, due = set(), set(), [], 0.0, {}, {}

    def occupy(way, size):
        end = now
        for axis, hops in enumerate(way[:3]):
            both = abs(hops) * 2 == (NX, NY, NZ)[axis]
            for sign in (1, -1) if both else (1,) if hops > 0 else (-1,):
                if hops:
                    key = (axis, sign)
                    link[key] = max(now, link.get(key, 0.0)) + size * 2 / 1e5 * abs(hops) / (2 if both else 1)
                    end = max(end, link[key])
        return end + 0.6 * max(0, sum(abs(hops) for hops in way[:3]) - 1)

    def send_ready():
        for i, node in enumerate(nodes):
            if i not in due and all(d in done for d in node.deps):
                if node.way:
                    due[i] = occupy(node.way, node.size) + LATENCY
                    sent.add(i)
                    steps.append(("send", i))
                else:
                    due[i] = now + node.pause

    send_ready()
    while len(done) < len(nodes):
        ready = [(due[i], i) for i in due if i not in done]
        arrived = [r for r in ready if r[1] in sent and r[0] <= now]
        tasks = [r[1] for r in ready if r[1] not in sent and r[0] <= now]
        if arrived:
            pick = min(arrived)[1]
        elif tasks:
            pick = min(tasks)
        else:
            now, pick = min(ready)
        steps.append(("take" if nodes[pick].way else "task", pick))
        done.add(pick)
        now += nodes[pick].cost
        send_ready()
    return steps


def halves(rows):
    low, count = rows
    return (low, count // 2), (low + count // 2, count // 2)


def tree(p_rows, q_rows):
    found = []

    def add(way, slot, rows, deps):
        found.append((way, slot, rows, list(deps)))
        return len(found) - 1

    def ring(offset_y, rows, deps, arrived):
        for way, half in ((1, 0), (-1, 1)):
            before = deps
            for step in range(4):
                part = rows if step < 3 else halves(rows)[half]
                before = [add((0, way), (offset_y, -way * step), part, before)]
                arrived.setdefault(way * 4 if step == 3 else -way * (step + 1), []).extend(before)

    arrived = {}
    ring(0, p_rows, [], arrived)
    arrived = {0: [], 4: arrived.pop(4) + arrived.pop(-4), **arrived}
    for offset_z in (4, 3, -3, 2, -2, 1, -1, 0):
        up = add((1, 0), (0, offset_z), p_rows, arrived[offset_z])
        down = add((-1, 0), (0, offset_z), p_rows, arrived[offset_z])
        add((1, 0), (-1, offset_z), halves(p_rows)[0], [up])
        add((-1, 0), (1, offset_z), halves(p_rows)[1], [down])
    up = add((1, 0), (0, 0), q_rows, [])
    down = add((-1, 0), (0, 0), q_rows, [])
    far = [add((1, 0), (-1, 0), halves(q_rows)[0], [up]), add((-1, 0), (1, 0), halves(q_rows)[1], [down])]
    for offset_y, deps in ((0, []), (-1, [up]), (1, [down]), (2, far)):
        ring(offset_y, q_rows, deps, {})
    return found


def kernel(
    routes_ref, gains_ref, tok_ref, gate_ref, up_ref, down_ref, out_ref,
    weights, downs, tiles, wide, sliced, chunked, near, acc, pick, blend, fold, mix,
    sent_rows, got_rows, back_rows, turned, part, part_in, cross, cross_in, over, over_in, over_last, last_in,
    sends, recvs, b_send, b_recv, w_own,
):
    own_e, own_t = lax.axis_index("expert"), lax.axis_index("tensor")
    x, c = lax.div(own_e, 2), lax.rem(own_e, 2)
    y, z = lax.div(own_t, NZ), lax.rem(own_t, NZ)

    def slot(dy, dz):
        return lax.rem(y + dy + NY, NY) * NZ + lax.rem(z + dz + NZ, NZ)

    def device(dx, dy, dz, dc=0):
        return (lax.rem(x + dx + NX, NX) * 2 + (1 - c if dc else c), slot(dy, dz))

    barrier = pltpu.get_barrier_semaphore()
    for dx, dc in PEERS[1:]:
        pl.semaphore_signal(barrier, inc=1, device_id=device(dx, 0, 0, dc), device_id_type=MESH)

    def greet(k, carry):
        pl.semaphore_signal(barrier, inc=1, device_id=device(0, lax.div(k, NZ), lax.rem(k, NZ)), device_id_type=MESH)
        return carry

    lax.fori_loop(1, NT, greet, 0)

    areas = (pl.ds(YZ_COLS, D - YZ_COLS), pl.ds(0, YZ_COLS))

    def own_copy(number):
        if number < 4:
            area, which = areas[number // 2], number % 2
            return pltpu.make_async_copy(
                (gate_ref, up_ref)[which].at[area], weights.at[which, area], w_own.at[number]
            )
        return pltpu.make_async_copy(down_ref, downs, w_own.at[number])

    for number in range(5):
        own_copy(number).start()

    nodes = []

    def message(way, size, src, dst, deps=(), act=None, cost=0.04, bundle=None, sender=0):
        nodes.append(Node(deps, cost, act, way, size, src, dst, bundle=bundle, sender=sender))
        return len(nodes) - 1

    def task(act, deps, cost, pause=0.0):
        nodes.append(Node(deps, cost, act, pause=pause))
        return len(nodes) - 1

    def sign(row, column):
        common = row & column
        common = common ^ (common >> 4)
        common = common ^ (common >> 2)
        common = common ^ (common >> 1)
        return (1 - 2 * (common & 1)).astype(F32)

    def iotas(rows, columns):
        shape = (rows, columns)
        return lax.broadcasted_iota(jnp.int32, shape, 0), lax.broadcasted_iota(jnp.int32, shape, 1)

    def lands(dx, dc):
        return PEERS.index((-dx % 4, dc))

    def peer_way(number):
        dx, dc = PEERS[number]
        return (-1 if dx == 3 else dx, 0, 0, dc)

    def tables():
        row, column = iotas(TOK, TOK)
        earlier = (row < column).astype(F32).astype(BF16)
        slots = iotas(CAP, TOK)[0].astype(F32)
        first, second = routes_ref[0:1, :], routes_ref[1:2, :]
        gain_1, gain_2 = gains_ref[0:1, :].astype(F32), gains_ref[1:2, :].astype(F32)
        for number, (dx, dc) in enumerate(PEERS):
            expert = device(dx, 0, 0, dc)[0]
            is_1, is_2 = (first == expert).astype(F32), (second == expert).astype(F32)
            named = is_1 + is_2
            place = jnp.dot(
                jnp.broadcast_to(named, (16, TOK)).astype(BF16), earlier, preferred_element_type=F32
            )[0:1]
            hit = jnp.where(slots == place, 1.0, 0.0) * named
            area = slice(number * CAP, (number + 1) * CAP)
            pick[area, :] = hit.astype(BF16)
            blend[area, :] = (hit * ((is_1 * gain_1 + is_2 * gain_2) * (1.0 / 16.0))).astype(BF16)

    def slice_rows():
        columns = pl.ds(pl.multiple_of(own_t * 128, 128), 128)
        sliced[...] = jnp.dot(pick[...], tok_ref[:, columns], preferred_element_type=F32).astype(BF16)

    def chunk_rows(low, high):
        for k in range(4):
            columns = tok_ref[:, YZ_COLS + 512 * k : YZ_COLS + 512 * (k + 1)]
            area = slice(low * CAP, high * CAP)
            rows = jnp.dot(pick[area, :], columns, preferred_element_type=F32).astype(BF16)
            for number in range(low, high):
                piece = rows[(number - low) * CAP : (number - low + 1) * CAP]
                if number == 0:
                    wide[k, 0:CAP, :] = piece
                else:
                    chunked[k, number] = piece

    def near_rows():
        for t in range(NT):
            columns = tok_ref[:, t * 128 : (t + 1) * 128]
            rows = jnp.dot(pick[0 : 2 * CAP, :], columns, preferred_element_type=F32).astype(BF16)
            tiles[t, 0:CAP, :] = rows[0:CAP]
            near[t] = rows[CAP : 2 * CAP]

    tables()
    slice_rows()
    chunk_rows(0, 8)
    near_task = task(near_rows, [], 0.5)

    slices, chunk_nodes = [], []
    for number in (2, 3, 4, 5, 6, 7):
        slices.append(message(
            peer_way(number), 16384,
            lambda number=number: sliced.at[pl.ds(number * CAP, CAP)],
            lambda number=number: tiles.at[own_t, pl.ds(lands(*PEERS[number]) * CAP, CAP)],
            bundle="slices",
        ))
    for k in range(4):
        chunk_nodes.append([
            message(
                peer_way(number), 65536,
                lambda k=k, number=number: chunked.at[k, number],
                lambda k=k, number=number: wide.at[k, pl.ds(lands(*PEERS[number]) * CAP, CAP)],
                bundle=("chunk", k),
            )
            for number in (2, 3, 4, 5, 6, 7, 1)
        ])
    near_node = message(
        (0, 0, 0, 1), 524288, lambda: near, lambda: tiles.at[pl.ds(0, NT), pl.ds(CAP, CAP)], [near_task]
    )
    group_nodes = [list(slices), [], [], []]
    base = len(nodes)
    for (dy, dz), (sy, sz), (low, count), deps in tree(*GATHER):
        def ref(sy=sy, sz=sz, low=low, count=count):
            return tiles.at[slot(sy, sz), pl.ds(low, count)]

        number = message((0, dy, dz), count * 256, ref, ref, [base + d for d in deps] if deps else slices, sender=1)
        group_nodes[(sy - dy) % 4].append(number)

    def fold_signs():
        fold[...] = sign(*iotas(HID, HID)).astype(BF16)

    def mix_signs(low):
        row, column = iotas(2 * CAP, 2 * HID)
        row = row + low
        mix[low : low + 2 * CAP, :] = jnp.where(
            (row & 15) == (column & 15), sign(row >> 4, column >> 4), 0.0
        ).astype(BF16)

    fold_task = task(fold_signs, [near_task], 0.1)
    mix_tasks = [task(lambda n=n: mix_signs(n * 2 * CAP), [fold_task], 0.05) for n in range(4)]

    def weights_wait(low):
        own_copy(low).wait()
        own_copy(low + 1).wait()

    wide_weights = task(lambda: weights_wait(0), [near_task], 0.02)
    tile_weights = task(lambda: weights_wait(2), [wide_weights], 0.02)

    started = []

    def accumulate(rows, low, count):
        fresh = not started
        started.append(low)
        for which in range(2):
            term = jnp.dot(rows, weights[which, pl.ds(low, count), :], preferred_element_type=F32)
            acc[which] = term if fresh else acc[which] + term

    def group_dot(group):
        base_y = lax.rem(y + group, NY)
        rows = jnp.concatenate([tiles[base_y * NZ + j] for j in range(NZ)], axis=1)
        accumulate(rows, base_y * 1024, 1024)

    def chunk_dot(k):
        accumulate(wide[k], YZ_COLS + 512 * k, 512)

    def hide():
        gate, up = acc[0], acc[1]
        hidden = (gate / (1.0 + jnp.exp(-gate)) * up).astype(BF16)
        sent_rows[...] = jnp.dot(hidden, fold[...], preferred_element_type=F32).astype(BF16)

    def piece(t):
        return pl.ds(pl.multiple_of(t * 16, 16), 16)

    def start_all(src, dst, turn):
        def start(k, carry):
            other = slot(lax.div(k, NZ), lax.rem(k, NZ))
            pltpu.make_async_remote_copy(
                src_ref=src.at[piece(other)], dst_ref=dst.at[piece(own_t)],
                send_sem=b_send.at[turn], recv_sem=b_recv.at[turn],
                device_id=(own_e, other), device_id_type=MESH,
            ).start()
            return carry

        lax.fori_loop(1, NT, start, 0)
        dst[piece(own_t), :] = src[piece(own_t), :]

    def all_of(ref, turn):
        area = ref.at[pl.ds(0, (NT - 1) * 16)]
        return pltpu.make_async_remote_copy(
            src_ref=area, dst_ref=area, send_sem=b_send.at[turn], recv_sem=b_recv.at[turn],
            device_id=(own_e, slot(0, 1)), device_id_type=MESH,
        )

    def rotate():
        all_of(got_rows, 0).wait_recv()
        values = jnp.dot(mix[...], got_rows[...], preferred_element_type=F32)
        back_rows[...] = (values * (1.0 / math.sqrt(NT * HID))).astype(BF16)
        start_all(back_rows, turned, 1)

    dots = [task(lambda k=k: chunk_dot(k), chunk_nodes[k] + [wide_weights], 0.5) for k in range(4)]
    for group in (0, 1, 3, 2):
        dots.append(task(
            lambda group=group: group_dot(group),
            group_nodes[group] + [tile_weights, near_node, near_task], 0.9,
        ))
    hidden_task = task(hide, dots + [fold_task], 1.0)
    gone = task(lambda: start_all(sent_rows, got_rows, 0), [hidden_task], 1.0)
    back = task(rotate, [gone] + mix_tasks, 1.5, B_PAUSE)
    come = task(lambda: all_of(turned, 1).wait_recv(), [back], 0.1, B_PAUSE)

    down_task = task(lambda: own_copy(4).wait(), [tile_weights], 0.02)

    def down_dot(group):
        base_y = lax.rem(y + group, NY)
        for side in range(2):
            columns = pl.ds(pl.multiple_of(base_y * 1536 + side * 768, 128), 768)
            values = jnp.dot(turned[...], downs[:, columns], preferred_element_type=F32).astype(BF16)
            for pair in range(2):
                q = 2 * side + pair
                low = 384 * pair
                part[base_y * NZ + 2 * q] = values[:, low : low + 128]
                part[base_y * NZ + 2 * q + 1] = values[:, low + 256 : low + 384]
                for number in range(8):
                    into = cross_in if number == 0 else cross
                    into[group, number, q] = values[number * CAP : (number + 1) * CAP, low + 128 : low + 256]

    group_task, cross_nodes = {}, {}
    for group in (2, 1, 3, 0):
        group_task[group] = task(lambda group=group: down_dot(group), [come, down_task], 0.8)
        cross_nodes[group] = [
            message(
                peer_way(n), 65536, lambda group=group, n=n: cross.at[group, n],
                lambda group=group, n=n: cross_in.at[group, lands(*PEERS[n])],
                [group_task[group]], bundle=("cross", group), sender=2,
            )
            for n in (2, 3, 4, 5, 6, 7, 1)
        ]

    def blended(rows):
        return lax.dot_general(blend[...], rows, (((0,), (0,)), ((), ())), preferred_element_type=F32)

    packed = {}
    for group in (2, 1, 3, 0):
        def pack(group=group):
            lane = iotas(CAP, 128)[1]
            for q in range(4):
                sums = blended(cross_in[group, 0:8, q].reshape(8 * CAP, 128))
                top, low = sums[0:CAP], sums[CAP:TOK]
                over[group, 2 * q] = jnp.where(lane < 64, top, pltpu.roll(low, 64, 1)).astype(BF16)
                over[group, 2 * q + 1] = jnp.where(lane < 64, pltpu.roll(top, 64, 1), low).astype(BF16)

        packed[group] = task(pack, cross_nodes[group] + [group_task[group]], 0.4)

    over_nodes = [
        message(
            (0, -1 if group == 3 else group, 0), 131072, lambda group=group: over.at[group],
            lambda group=group: over_in.at[group - 1], [packed[group]], sender=2,
        )
        for group in (2, 1, 3)
    ]

    def add_over():
        for n in range(NZ):
            sums = over[0, n].astype(F32)
            for index in range(3):
                sums = sums + over_in[index, n].astype(F32)
            over[0, n] = sums.astype(BF16)

    over_task = task(add_over, over_nodes + [packed[0]], 0.3)
    ends = [
        message(
            (0, 0, dz), 16384, lambda dz=dz: over.at[0, lax.rem(z + dz + NZ, NZ)],
            lambda dz=dz: over_last.at[dz % NZ - 1], [over_task], bundle="over", sender=2,
        )
        for dz in (4, 3, -3, 2, -2, 1, -1)
    ]

    total, base = 0, len(nodes)
    reduction = tree(*REDUCE)
    roots = [group_task[0]]
    for number, ((dy, dz), (sy, sz), (low, count), deps) in enumerate(reduction):
        def src(sy=sy, sz=sz, dy=dy, dz=dz, low=low, count=count):
            return part.at[slot(sy - dy, sz - dz), pl.ds(low, count)]

        def dst(total=total, count=count):
            return part_in.at[pl.ds(total, count)]

        def act(sy=sy, sz=sz, low=low, count=count, total=total):
            here = slot(sy, sz)
            part[here, low : low + count, :] = part[here, low : low + count, :] + part_in[total : total + count, :]

        children = [base + n for n, other in enumerate(reduction) if number in other[3]]
        if not deps:
            roots.append(base + number)
        needs = [group_task[(sy - dy) % 4], group_task[sy % 4]]
        message((0, -dy, -dz), count * 256, src, dst, children + needs, act, count / 4000, sender=3)
        total += count
    lasts = [
        message(
            peer_way(n), 16384, lambda n=n: part.at[own_t, pl.ds(n * CAP, CAP)],
            lambda n=n: last_in.at[pl.ds(lands(*PEERS[n]) * CAP, CAP)], roots, bundle="last", sender=2,
        )
        for n in (2, 3, 4, 5, 6, 7, 1)
    ]

    def store():
        last_in[0:CAP, :] = part[own_t, 0:CAP, :]
        summed = blended(last_in[...])
        rolled = pltpu.roll(summed, 64, 1)
        extra = over[0, z].astype(F32)
        for index in range(NZ - 1):
            extra = extra + over_last[index].astype(F32)
        extra = jnp.concatenate([extra, pltpu.roll(extra, 64, 1)], axis=0)
        odd = lax.rem(own_t, 2) == 1
        lane = iotas(TOK, 128)[1]
        left = jnp.where(odd, jnp.where(lane < 64, extra, rolled), summed)
        right = jnp.where(odd, rolled, extra)
        out_ref[:, 0:128] = left.astype(BF16)
        out_ref[:, 128:192] = right[:, 0:64].astype(BF16)

    task(store, lasts + ends, 0.2)

    marks = []
    for number, node in enumerate(nodes):
        if node.way:
            key = node.bundle or number
            if key not in marks:
                marks.append(key)

    def copy_of(number, src=None, dst=None):
        node = nodes[number]
        return pltpu.make_async_remote_copy(
            src_ref=src or node.src(), dst_ref=dst or node.dst(),
            send_sem=sends.at[node.sender], recv_sem=recvs.at[marks.index(node.bundle or number)],
            device_id=device(*node.way), device_id_type=MESH,
        )

    def rows_of(chosen):
        return part_in.at[pl.ds(0, sum(node.size for node in chosen) // 256)]

    pl.semaphore_wait(barrier, NT - 1 + 7)
    taken = {}
    for kind, number in steps_of(nodes):
        node = nodes[number]
        if kind == "send":
            copy_of(number).start()
            continue
        if kind == "take" and node.bundle:
            members = [other for other in nodes if other.bundle == node.bundle]
            taken[node.bundle] = taken.get(node.bundle, 0) + 1
            if taken[node.bundle] == len(members):
                area = rows_of(members)
                copy_of(number, area, area).wait_recv()
        elif kind == "take":
            copy_of(number).wait_recv()
        if node.act:
            node.act()

    for sender in range(4):
        chosen = [number for number, node in enumerate(nodes) if node.way and node.sender == sender]
        area = rows_of([nodes[number] for number in chosen])
        copy_of(chosen[0], area, area).wait_send()
    for turn in range(2):
        all_of(back_rows, turn).wait_send()


def shards(tokens, routes, gate_num, gate_weight, up_weight, down_weight):
    vmem, anywhere = pl.BlockSpec(memory_space=pltpu.VMEM), pl.BlockSpec(memory_space=pl.ANY)
    dma = pltpu.SemaphoreType.DMA
    return pl.pallas_call(
        kernel,
        out_shape=jax.ShapeDtypeStruct((TOK, 192), BF16),
        in_specs=[vmem, vmem, vmem, anywhere, anywhere, anywhere],
        out_specs=vmem,
        scratch_shapes=[
            pltpu.VMEM((2, D, HID), BF16),
            pltpu.VMEM((HID, D), BF16),
            pltpu.VMEM((NT, 8 * CAP, 128), BF16),
            pltpu.VMEM((4, 8 * CAP, 512), BF16),
            pltpu.VMEM((8 * CAP, 128), BF16),
            pltpu.VMEM((4, 8, CAP, 512), BF16),
            pltpu.VMEM((NT, CAP, 128), BF16),
            pltpu.VMEM((2, 8 * CAP, HID), F32),
            pltpu.VMEM((8 * CAP, TOK), BF16),
            pltpu.VMEM((8 * CAP, TOK), BF16),
            pltpu.VMEM((HID, HID), BF16),
            pltpu.VMEM((2 * HID, 2 * HID), BF16),
            pltpu.VMEM((8 * CAP, HID), BF16),
            pltpu.VMEM((8 * CAP, HID), BF16),
            pltpu.VMEM((8 * CAP, HID), BF16),
            pltpu.VMEM((8 * CAP, HID), BF16),
            pltpu.VMEM((NT, 8 * CAP, 128), BF16),
            pltpu.VMEM((15872, 128), BF16),
            pltpu.VMEM((4, 8, 4, CAP, 128), BF16),
            pltpu.VMEM((4, 8, 4, CAP, 128), BF16),
            pltpu.VMEM((4, NZ, CAP, 128), BF16),
            pltpu.VMEM((3, NZ, CAP, 128), BF16),
            pltpu.VMEM((NZ - 1, CAP, 128), BF16),
            pltpu.VMEM((8 * CAP, 128), BF16),
            dma((4,)), dma((168,)), dma((2,)), dma((2,)), dma((5,)),
        ],
        compiler_params=pltpu.CompilerParams(
            collective_id=0, has_side_effects=True, vmem_limit_bytes=60 * 2**20
        ),
        cost_estimate=pl.CostEstimate(flops=10**10, bytes_accessed=2 * 10**7, transcendentals=2**18),
        name="moe_layer",
    )(routes.T, gate_num.T, tokens, gate_weight[0], up_weight[0], down_weight[0])


def solution(mesh):
    placed = (
        P("expert", None),
        P("expert", None),
        P("expert", None),
        P("expert", None, "tensor"),
        P("expert", None, "tensor"),
        P("expert", "tensor", None),
    )
    return jax.shard_map(
        shards, mesh=mesh, in_specs=placed, out_specs=P("expert", "tensor"), check_vma=False
    )
```

```python
import math

import jax
import jax.numpy as jnp
from jax import lax
from jax.experimental import pallas as pl
from jax.experimental.pallas import tpu as pltpu
from jax.sharding import PartitionSpec as P

NX, NY, NZ, NT = 4, 4, 8, 32
CAP, TOK, D, HID = 64, 128, 6144, 256
YZ_COLS = NT * 128
MESH = pl.DeviceIdType.MESH
BF16, F32 = jnp.bfloat16, jnp.float32

PEERS = tuple((dx, dc) for dx in (0, 2, 1, 3) for dc in (0, 1))
GATHER = ((128, 256), (384, 128))
REDUCE = ((0, 256), (256, 256))
LATENCY, B_PAUSE = 1.6, 6.0


class Node:
    def __init__(self, deps, cost, act=None, way=None, size=0, src=None, dst=None, pause=0.0, bundle=None, sender=None):
        self.deps, self.cost, self.act, self.pause = list(deps), cost, act, pause
        self.way, self.size, self.src, self.dst, self.bundle, self.sender = way, size, src, dst, bundle, sender


def steps_of(nodes):
    done, sent, steps, now, link, due = set(), set(), [], 0.0, {}, {}

    def occupy(way, size):
        end = now
        for axis, hops in enumerate(way[:3]):
            both = abs(hops) * 2 == (NX, NY, NZ)[axis]
            for sign in (1, -1) if both else (1,) if hops > 0 else (-1,):
                if hops:
                    key = (axis, sign)
                    link[key] = max(now, link.get(key, 0.0)) + size * 2 / 1e5 * abs(hops) / (2 if both else 1)
                    end = max(end, link[key])
        return end + 0.6 * max(0, sum(abs(hops) for hops in way[:3]) - 1)

    def send_ready():
        for i, node in enumerate(nodes):
            if i not in due and all(d in done for d in node.deps):
                if node.way:
                    due[i] = occupy(node.way, node.size) + LATENCY
                    sent.add(i)
                    steps.append(("send", i))
                else:
                    due[i] = now + node.pause

    send_ready()
    while len(done) < len(nodes):
        ready = [(due[i], i) for i in due if i not in done]
        arrived = [r for r in ready if r[1] in sent and r[0] <= now]
        tasks = [r[1] for r in ready if r[1] not in sent and r[0] <= now]
        if arrived:
            pick = min(arrived)[1]
        elif tasks:
            pick = min(tasks)
        else:
            now, pick = min(ready)
        steps.append(("take" if nodes[pick].way else "task", pick))
        done.add(pick)
        now += nodes[pick].cost
        send_ready()
    return steps


def halves(rows):
    low, count = rows
    return (low, count // 2), (low + count // 2, count // 2)


def tree(p_rows, q_rows):
    found = []

    def add(way, slot, rows, deps):
        found.append((way, slot, rows, list(deps)))
        return len(found) - 1

    def ring(offset_y, rows, deps, arrived):
        for way, half in ((1, 0), (-1, 1)):
            before = deps
            for step in range(4):
                part = rows if step < 3 else halves(rows)[half]
                before = [add((0, way), (offset_y, -way * step), part, before)]
                arrived.setdefault(way * 4 if step == 3 else -way * (step + 1), []).extend(before)

    arrived = {}
    ring(0, p_rows, [], arrived)
    arrived = {0: [], 4: arrived.pop(4) + arrived.pop(-4), **arrived}
    for offset_z in (4, 3, -3, 2, -2, 1, -1, 0):
        up = add((1, 0), (0, offset_z), p_rows, arrived[offset_z])
        down = add((-1, 0), (0, offset_z), p_rows, arrived[offset_z])
        add((1, 0), (-1, offset_z), halves(p_rows)[0], [up])
        add((-1, 0), (1, offset_z), halves(p_rows)[1], [down])
    up = add((1, 0), (0, 0), q_rows, [])
    down = add((-1, 0), (0, 0), q_rows, [])
    far = [add((1, 0), (-1, 0), halves(q_rows)[0], [up]), add((-1, 0), (1, 0), halves(q_rows)[1], [down])]
    for offset_y, deps in ((0, []), (-1, [up]), (1, [down]), (2, far)):
        ring(offset_y, q_rows, deps, {})
    return found


def kernel(
    routes_ref, gains_ref, tok_ref, gate_ref, up_ref, down_ref, out_ref,
    weights, downs, tiles, wide, sliced, chunked, near, acc, pick, blend, fold, mix,
    sent_rows, got_rows, back_rows, turned, part, part_in, cross, cross_in, over, over_in, over_last, last_in,
    sends, recvs, b_send, b_recv, w_own,
):
    own_e, own_t = lax.axis_index("expert"), lax.axis_index("tensor")
    x, c = lax.div(own_e, 2), lax.rem(own_e, 2)
    y, z = lax.div(own_t, NZ), lax.rem(own_t, NZ)

    def slot(dy, dz):
        return lax.rem(y + dy + NY, NY) * NZ + lax.rem(z + dz + NZ, NZ)

    def device(dx, dy, dz, dc=0):
        return (lax.rem(x + dx + NX, NX) * 2 + (1 - c if dc else c), slot(dy, dz))

    barrier = pltpu.get_barrier_semaphore()
    for dx, dc in PEERS[1:]:
        pl.semaphore_signal(barrier, inc=1, device_id=device(dx, 0, 0, dc), device_id_type=MESH)

    def greet(k, carry):
        pl.semaphore_signal(barrier, inc=1, device_id=device(0, lax.div(k, NZ), lax.rem(k, NZ)), device_id_type=MESH)
        return carry

    lax.fori_loop(1, NT, greet, 0)

    areas = (pl.ds(YZ_COLS, D - YZ_COLS), pl.ds(0, YZ_COLS))

    def own_copy(number):
        if number < 4:
            area, which = areas[number // 2], number % 2
            return pltpu.make_async_copy(
                (gate_ref, up_ref)[which].at[area], weights.at[which, area], w_own.at[number]
            )
        return pltpu.make_async_copy(down_ref, downs, w_own.at[number])

    for number in range(5):
        own_copy(number).start()

    nodes = []

    def message(way, size, src, dst, deps=(), act=None, cost=0.04, bundle=None, sender=0):
        nodes.append(Node(deps, cost, act, way, size, src, dst, bundle=bundle, sender=sender))
        return len(nodes) - 1

    def task(act, deps, cost, pause=0.0):
        nodes.append(Node(deps, cost, act, pause=pause))
        return len(nodes) - 1

    def sign(row, column):
        common = row & column
        common = common ^ (common >> 4)
        common = common ^ (common >> 2)
        common = common ^ (common >> 1)
        return (1 - 2 * (common & 1)).astype(F32)

    def iotas(rows, columns):
        shape = (rows, columns)
        return lax.broadcasted_iota(jnp.int32, shape, 0), lax.broadcasted_iota(jnp.int32, shape, 1)

    def lands(dx, dc):
        return PEERS.index((-dx % 4, dc))

    def peer_way(number):
        dx, dc = PEERS[number]
        return (-1 if dx == 3 else dx, 0, 0, dc)

    def tables():
        row, column = iotas(TOK, TOK)
        earlier = (row < column).astype(F32).astype(BF16)
        slots = iotas(CAP, TOK)[0].astype(F32)
        first, second = routes_ref[0:1, :], routes_ref[1:2, :]
        gain_1, gain_2 = gains_ref[0:1, :].astype(F32), gains_ref[1:2, :].astype(F32)
        for number, (dx, dc) in enumerate(PEERS):
            expert = device(dx, 0, 0, dc)[0]
            is_1, is_2 = (first == expert).astype(F32), (second == expert).astype(F32)
            named = is_1 + is_2
            place = jnp.dot(
                jnp.broadcast_to(named, (16, TOK)).astype(BF16), earlier, preferred_element_type=F32
            )[0:1]
            hit = jnp.where(slots == place, 1.0, 0.0) * named
            area = slice(number * CAP, (number + 1) * CAP)
            pick[area, :] = hit.astype(BF16)
            blend[area, :] = (hit * ((is_1 * gain_1 + is_2 * gain_2) * (1.0 / 16.0))).astype(BF16)

    def slice_rows():
        columns = pl.ds(pl.multiple_of(own_t * 128, 128), 128)
        sliced[...] = jnp.dot(pick[...], tok_ref[:, columns], preferred_element_type=F32).astype(BF16)

    def chunk_rows(k):
        columns = tok_ref[:, YZ_COLS + 512 * k : YZ_COLS + 512 * (k + 1)]
        rows = jnp.dot(pick[...], columns, preferred_element_type=F32).astype(BF16)
        wide[k, 0:CAP, :] = rows[0:CAP]
        for number in range(1, 8):
            chunked[k, number] = rows[number * CAP : (number + 1) * CAP]

    def near_rows():
        for t in range(NT):
            columns = tok_ref[:, t * 128 : (t + 1) * 128]
            rows = jnp.dot(pick[0 : 2 * CAP, :], columns, preferred_element_type=F32).astype(BF16)
            tiles[t, 0:CAP, :] = rows[0:CAP]
            near[t] = rows[CAP : 2 * CAP]

    tables()
    slice_rows()
    chunk_tasks = [task(lambda k=k: chunk_rows(k), [], 0.25) for k in range(4)]
    near_task = task(near_rows, chunk_tasks, 0.5)

    slices, chunk_nodes = [], []
    for number in (2, 3, 4, 5, 6, 7):
        slices.append(message(
            peer_way(number), 16384,
            lambda number=number: sliced.at[pl.ds(number * CAP, CAP)],
            lambda number=number: tiles.at[own_t, pl.ds(lands(*PEERS[number]) * CAP, CAP)],
            bundle="slices",
        ))
    for k in range(4):
        chunk_nodes.append([
            message(
                peer_way(number), 65536,
                lambda k=k, number=number: chunked.at[k, number],
                lambda k=k, number=number: wide.at[k, pl.ds(lands(*PEERS[number]) * CAP, CAP)],
                [chunk_tasks[k]] + (chunk_nodes[k - 2] if k > 1 else []), bundle=("chunk", k),
            )
            for number in (2, 3, 4, 5, 6, 7, 1)
        ])
    near_node = message(
        (0, 0, 0, 1), 524288, lambda: near, lambda: tiles.at[pl.ds(0, NT), pl.ds(CAP, CAP)], [near_task]
    )
    group_nodes = [list(slices), [], [], []]
    base = len(nodes)
    for (dy, dz), (sy, sz), (low, count), deps in tree(*GATHER):
        def ref(sy=sy, sz=sz, low=low, count=count):
            return tiles.at[slot(sy, sz), pl.ds(low, count)]

        number = message((0, dy, dz), count * 256, ref, ref, [base + d for d in deps] if deps else slices, sender=1)
        group_nodes[(sy - dy) % 4].append(number)

    def fold_signs():
        fold[...] = sign(*iotas(HID, HID)).astype(BF16)

    def mix_signs(low):
        row, column = iotas(2 * CAP, 2 * HID)
        row = row + low
        mix[low : low + 2 * CAP, :] = jnp.where(
            (row & 15) == (column & 15), sign(row >> 4, column >> 4), 0.0
        ).astype(BF16)

    fold_task = task(fold_signs, [near_task], 0.1)
    mix_tasks = [task(lambda n=n: mix_signs(n * 2 * CAP), [fold_task], 0.05) for n in range(4)]

    def weights_wait(low):
        own_copy(low).wait()
        own_copy(low + 1).wait()

    wide_weights = task(lambda: weights_wait(0), [near_task], 0.02)
    tile_weights = task(lambda: weights_wait(2), [wide_weights], 0.02)

    started = []

    def accumulate(rows, low, count):
        fresh = not started
        started.append(low)
        for which in range(2):
            term = jnp.dot(rows, weights[which, pl.ds(low, count), :], preferred_element_type=F32)
            acc[which] = term if fresh else acc[which] + term

    def group_dot(group):
        base_y = lax.rem(y + group, NY)
        rows = jnp.concatenate([tiles[base_y * NZ + j] for j in range(NZ)], axis=1)
        accumulate(rows, base_y * 1024, 1024)

    def chunk_dot(k):
        accumulate(wide[k], YZ_COLS + 512 * k, 512)

    def hide():
        gate, up = acc[0], acc[1]
        hidden = (gate / (1.0 + jnp.exp(-gate)) * up).astype(BF16)
        sent_rows[...] = jnp.dot(hidden, fold[...], preferred_element_type=F32).astype(BF16)

    def piece(t):
        return pl.ds(pl.multiple_of(t * 16, 16), 16)

    def start_all(src, dst, turn):
        for dy, dz in sorted(
            [(dy, dz) for dy in range(NY) for dz in range(NZ) if dy or dz],
            key=lambda d: -min(d[0], NY - d[0]) - min(d[1], NZ - d[1]),
        ):
            other = slot(dy, dz)
            pltpu.make_async_remote_copy(
                src_ref=src.at[piece(other)], dst_ref=dst.at[piece(own_t)],
                send_sem=b_send.at[turn], recv_sem=b_recv.at[turn],
                device_id=(own_e, other), device_id_type=MESH,
            ).start()
        dst[piece(own_t), :] = src[piece(own_t), :]

    def all_of(ref, turn):
        area = ref.at[pl.ds(0, (NT - 1) * 16)]
        return pltpu.make_async_remote_copy(
            src_ref=area, dst_ref=area, send_sem=b_send.at[turn], recv_sem=b_recv.at[turn],
            device_id=(own_e, slot(0, 1)), device_id_type=MESH,
        )

    def rotate():
        all_of(got_rows, 0).wait_recv()
        values = jnp.dot(mix[...], got_rows[...], preferred_element_type=F32)
        back_rows[...] = (values * (1.0 / math.sqrt(NT * HID))).astype(BF16)
        start_all(back_rows, turned, 1)

    dots = [task(lambda k=k: chunk_dot(k), chunk_nodes[k] + [chunk_tasks[k], wide_weights], 0.5) for k in range(4)]
    for group in (0, 1, 3, 2):
        dots.append(task(
            lambda group=group: group_dot(group),
            group_nodes[group] + [tile_weights, near_node, near_task], 0.9,
        ))
    hidden_task = task(hide, dots + [fold_task], 1.0)
    gone = task(lambda: start_all(sent_rows, got_rows, 0), [hidden_task], 1.0)
    back = task(rotate, [gone] + mix_tasks, 1.5, B_PAUSE)
    come = task(lambda: all_of(turned, 1).wait_recv(), [back], 0.1, B_PAUSE)

    down_task = task(lambda: own_copy(4).wait(), [tile_weights], 0.02)

    def down_dot(group):
        base_y = lax.rem(y + group, NY)
        for side in range(2):
            columns = pl.ds(pl.multiple_of(base_y * 1536 + side * 768, 128), 768)
            values = jnp.dot(turned[...], downs[:, columns], preferred_element_type=F32).astype(BF16)
            for pair in range(2):
                q = 2 * side + pair
                low = 384 * pair
                part[base_y * NZ + 2 * q] = values[:, low : low + 128]
                part[base_y * NZ + 2 * q + 1] = values[:, low + 256 : low + 384]
                for number in range(8):
                    into = cross_in if number == 0 else cross
                    into[group, number, q] = values[number * CAP : (number + 1) * CAP, low + 128 : low + 256]

    group_task, cross_nodes = {}, {}
    for group in (2, 1, 3, 0):
        group_task[group] = task(lambda group=group: down_dot(group), [come, down_task], 0.8)
        cross_nodes[group] = [
            message(
                peer_way(n), 65536, lambda group=group, n=n: cross.at[group, n],
                lambda group=group, n=n: cross_in.at[group, lands(*PEERS[n])],
                [group_task[group]], bundle=("cross", group), sender=2,
            )
            for n in (2, 3, 4, 5, 6, 7, 1)
        ]

    def blended(rows):
        return lax.dot_general(rows, blend[...], (((0,), (0,)), ((), ())), preferred_element_type=F32)

    packed = {}
    for group in (2, 1, 3, 0):
        def pack(group=group):
            for q in range(4):
                sums = blended(cross_in[group, 0:8, q].reshape(8 * CAP, 128)).astype(BF16)
                over[group, 2 * q] = sums[0:CAP]
                over[group, 2 * q + 1] = sums[CAP : 2 * CAP]

        packed[group] = task(pack, cross_nodes[group] + [group_task[group]], 0.4)

    over_nodes = [
        message(
            (0, -1 if group == 3 else group, 0), 131072, lambda group=group: over.at[group],
            lambda group=group: over_in.at[group - 1], [packed[group]], sender=2,
        )
        for group in (2, 1, 3)
    ]

    def add_over():
        for n in range(NZ):
            sums = over[0, n].astype(F32)
            for index in range(3):
                sums = sums + over_in[index, n].astype(F32)
            over[0, n] = sums.astype(BF16)

    over_task = task(add_over, over_nodes + [packed[0]], 0.3)
    ends = [
        message(
            (0, 0, dz), 16384, lambda dz=dz: over.at[0, lax.rem(z + dz + NZ, NZ)],
            lambda dz=dz: over_last.at[dz % NZ - 1], [over_task], bundle="over", sender=2,
        )
        for dz in (4, 3, -3, 2, -2, 1, -1)
    ]

    total, base = 0, len(nodes)
    reduction = tree(*REDUCE)
    roots = {False: [group_task[0]], True: [group_task[0]]}
    for number, ((dy, dz), (sy, sz), (low, count), deps) in enumerate(reduction):
        def src(sy=sy, sz=sz, dy=dy, dz=dz, low=low, count=count):
            return part.at[slot(sy - dy, sz - dz), pl.ds(low, count)]

        def dst(total=total, count=count):
            return part_in.at[pl.ds(total, count)]

        def act(sy=sy, sz=sz, low=low, count=count, total=total):
            here = slot(sy, sz)
            part[here, low : low + count, :] = part[here, low : low + count, :] + part_in[total : total + count, :]

        children = [base + n for n, other in enumerate(reduction) if number in other[3]]
        if not deps:
            roots[low >= REDUCE[1][0]].append(base + number)
        needs = [group_task[(sy - dy) % 4], group_task[sy % 4]]
        message((0, -dy, -dz), count * 256, src, dst, children + needs, act, count / 4000, sender=3)
        total += count
    lasts = [
        message(
            peer_way(n), 16384, lambda n=n: part.at[own_t, pl.ds(n * CAP, CAP)],
            lambda n=n: last_in.at[pl.ds(lands(*PEERS[n]) * CAP, CAP)], roots[n > 3], bundle="last", sender=2,
        )
        for n in (2, 3, 4, 5, 6, 7, 1)
    ]

    def store():
        last_in[0:CAP, :] = part[own_t, 0:CAP, :]
        summed = blended(last_in[...])
        odd = lax.rem(own_t, 2)
        out_ref[pl.ds(pl.multiple_of(odd * CAP, CAP), TOK), :] = summed.astype(BF16)
        extra = over[0, z].astype(F32)
        for index in range(NZ - 1):
            extra = extra + over_last[index].astype(F32)
        out_ref[pl.ds(pl.multiple_of((1 - odd) * TOK, CAP), CAP), :] = extra.astype(BF16)

    task(store, lasts + ends, 0.2)

    marks = []
    for number, node in enumerate(nodes):
        if node.way:
            key = node.bundle or number
            if key not in marks:
                marks.append(key)

    def copy_of(number, src=None, dst=None):
        node = nodes[number]
        return pltpu.make_async_remote_copy(
            src_ref=src or node.src(), dst_ref=dst or node.dst(),
            send_sem=sends.at[node.sender], recv_sem=recvs.at[marks.index(node.bundle or number)],
            device_id=device(*node.way), device_id_type=MESH,
        )

    def rows_of(chosen):
        return part_in.at[pl.ds(0, sum(node.size for node in chosen) // 256)]

    pl.semaphore_wait(barrier, NT - 1 + 7)
    taken = {}
    for kind, number in steps_of(nodes):
        node = nodes[number]
        if kind == "send":
            copy_of(number).start()
            continue
        if kind == "take" and node.bundle:
            members = [other for other in nodes if other.bundle == node.bundle]
            taken[node.bundle] = taken.get(node.bundle, 0) + 1
            if taken[node.bundle] == len(members):
                area = rows_of(members)
                copy_of(number, area, area).wait_recv()
        elif kind == "take":
            copy_of(number).wait_recv()
        if node.act:
            node.act()

    for sender in range(4):
        chosen = [number for number, node in enumerate(nodes) if node.way and node.sender == sender]
        area = rows_of([nodes[number] for number in chosen])
        copy_of(chosen[0], area, area).wait_send()
    for turn in range(2):
        all_of(back_rows, turn).wait_send()


def shards(tokens, routes, gate_num, gate_weight, up_weight, down_weight):
    vmem, anywhere = pl.BlockSpec(memory_space=pltpu.VMEM), pl.BlockSpec(memory_space=pl.ANY)
    dma = pltpu.SemaphoreType.DMA
    return pl.pallas_call(
        kernel,
        out_shape=jax.ShapeDtypeStruct((192, TOK), BF16),
        in_specs=[vmem, vmem, vmem, anywhere, anywhere, anywhere],
        out_specs=vmem,
        scratch_shapes=[
            pltpu.VMEM((2, D, HID), BF16),
            pltpu.VMEM((HID, D), BF16),
            pltpu.VMEM((NT, 8 * CAP, 128), BF16),
            pltpu.VMEM((4, 8 * CAP, 512), BF16),
            pltpu.VMEM((8 * CAP, 128), BF16),
            pltpu.VMEM((4, 8, CAP, 512), BF16),
            pltpu.VMEM((NT, CAP, 128), BF16),
            pltpu.VMEM((2, 8 * CAP, HID), F32),
            pltpu.VMEM((8 * CAP, TOK), BF16),
            pltpu.VMEM((8 * CAP, TOK), BF16),
            pltpu.VMEM((HID, HID), BF16),
            pltpu.VMEM((2 * HID, 2 * HID), BF16),
            pltpu.VMEM((8 * CAP, HID), BF16),
            pltpu.VMEM((8 * CAP, HID), BF16),
            pltpu.VMEM((8 * CAP, HID), BF16),
            pltpu.VMEM((8 * CAP, HID), BF16),
            pltpu.VMEM((NT, 8 * CAP, 128), BF16),
            pltpu.VMEM((15872, 128), BF16),
            pltpu.VMEM((4, 8, 4, CAP, 128), BF16),
            pltpu.VMEM((4, 8, 4, CAP, 128), BF16),
            pltpu.VMEM((4, NZ, CAP, 128), BF16),
            pltpu.VMEM((3, NZ, CAP, 128), BF16),
            pltpu.VMEM((NZ - 1, CAP, 128), BF16),
            pltpu.VMEM((8 * CAP, 128), BF16),
            dma((4,)), dma((168,)), dma((2,)), dma((2,)), dma((5,)),
        ],
        compiler_params=pltpu.CompilerParams(
            collective_id=0, has_side_effects=True, vmem_limit_bytes=60 * 2**20
        ),
        cost_estimate=pl.CostEstimate(flops=10**10, bytes_accessed=2 * 10**7, transcendentals=2**18),
        name="moe_layer",
    )(routes.T, gate_num.T, tokens, gate_weight[0], up_weight[0], down_weight[0]).T


def solution(mesh):
    placed = (
        P("expert", None),
        P("expert", None),
        P("expert", None),
        P("expert", None, "tensor"),
        P("expert", None, "tensor"),
        P("expert", "tensor", None),
    )
    return jax.shard_map(
        shards, mesh=mesh, in_specs=placed, out_specs=P("expert", "tensor"), check_vma=False
    )
```

```python
import math

import jax
import jax.numpy as jnp
from jax import lax
from jax.experimental import pallas as pl
from jax.experimental.pallas import tpu as pltpu
from jax.sharding import PartitionSpec as P

NX, NY, NZ, NT = 4, 4, 8, 32
CAP, TOK, D, HID = 64, 128, 6144, 256
YZ_COLS = NT * 128
MESH = pl.DeviceIdType.MESH
BF16, F32 = jnp.bfloat16, jnp.float32

PEERS = tuple((dx, dc) for dx in (0, 2, 1, 3) for dc in (0, 1))
GATHER = ((128, 256), (384, 128))
REDUCE = ((0, 256), (256, 256))
LATENCY, B_PAUSE = 1.6, 6.0


class Node:
    def __init__(self, deps, cost, act=None, way=None, size=0, src=None, dst=None, pause=0.0, bundle=None, sender=None, mark=None):
        self.deps, self.cost, self.act, self.pause = list(deps), cost, act, pause
        self.way, self.size, self.src, self.dst, self.bundle, self.sender = way, size, src, dst, bundle, sender
        self.mark = mark or bundle


def steps_of(nodes):
    done, sent, steps, now, link, due = set(), set(), [], 0.0, {}, {}

    def occupy(way, size):
        end = now
        for axis, hops in enumerate(way[:3]):
            both = abs(hops) * 2 == (NX, NY, NZ)[axis]
            for sign in (1, -1) if both else (1,) if hops > 0 else (-1,):
                if hops:
                    key = (axis, sign)
                    link[key] = max(now, link.get(key, 0.0)) + size * 2 / 1e5 * abs(hops) / (2 if both else 1)
                    end = max(end, link[key])
        return end + 0.6 * max(0, sum(abs(hops) for hops in way[:3]) - 1)

    def send_ready():
        for i, node in enumerate(nodes):
            if i not in due and all(d in done for d in node.deps):
                if node.way:
                    due[i] = occupy(node.way, node.size) + LATENCY
                    sent.add(i)
                    steps.append(("send", i))
                else:
                    due[i] = now + node.pause

    send_ready()
    while len(done) < len(nodes):
        ready = [(due[i], i) for i in due if i not in done]
        arrived = [r for r in ready if r[1] in sent and r[0] <= now]
        tasks = [r[1] for r in ready if r[1] not in sent and r[0] <= now]
        if arrived:
            pick = min(arrived)[1]
        elif tasks:
            pick = min(tasks)
        else:
            now, pick = min(ready)
        steps.append(("take" if nodes[pick].way else "task", pick))
        done.add(pick)
        now += nodes[pick].cost
        send_ready()
    return steps


def halves(rows):
    low, count = rows
    return (low, count // 2), (low + count // 2, count // 2)


def tree(p_rows, q_rows):
    found = []

    def add(way, slot, rows, deps):
        found.append((way, slot, rows, list(deps)))
        return len(found) - 1

    def ring(offset_y, rows, deps, arrived):
        for way, half in ((1, 0), (-1, 1)):
            before = deps
            for step in range(4):
                part = rows if step < 3 else halves(rows)[half]
                before = [add((0, way), (offset_y, -way * step), part, before)]
                arrived.setdefault(way * 4 if step == 3 else -way * (step + 1), []).extend(before)

    arrived = {}
    ring(0, p_rows, [], arrived)
    arrived = {0: [], 4: arrived.pop(4) + arrived.pop(-4), **arrived}
    for offset_z in (4, 3, -3, 2, -2, 1, -1, 0):
        up = add((1, 0), (0, offset_z), p_rows, arrived[offset_z])
        down = add((-1, 0), (0, offset_z), p_rows, arrived[offset_z])
        add((1, 0), (-1, offset_z), halves(p_rows)[0], [up])
        add((-1, 0), (1, offset_z), halves(p_rows)[1], [down])
    up = add((1, 0), (0, 0), q_rows, [])
    down = add((-1, 0), (0, 0), q_rows, [])
    far = [add((1, 0), (-1, 0), halves(q_rows)[0], [up]), add((-1, 0), (1, 0), halves(q_rows)[1], [down])]
    for offset_y, deps in ((0, []), (-1, [up]), (1, [down]), (2, far)):
        ring(offset_y, q_rows, deps, {})
    return found


def kernel(
    routes_ref, gains_ref, tok_ref, gate_ref, up_ref, down_ref, out_ref,
    weights, downs, tiles, wide, sliced, chunked, near, acc, pick, blend, fold, mix,
    sent_rows, got_rows, back_rows, turned, part, part_in, cross, cross_in, over, over_in, over_last, last_in,
    sends, recvs, b_send, b_recv, w_own,
):
    own_e, own_t = lax.axis_index("expert"), lax.axis_index("tensor")
    x, c = lax.div(own_e, 2), lax.rem(own_e, 2)
    y, z = lax.div(own_t, NZ), lax.rem(own_t, NZ)

    def slot(dy, dz):
        return lax.rem(y + dy + NY, NY) * NZ + lax.rem(z + dz + NZ, NZ)

    def device(dx, dy, dz, dc=0):
        return (lax.rem(x + dx + NX, NX) * 2 + (1 - c if dc else c), slot(dy, dz))

    barrier = pltpu.get_barrier_semaphore()
    for dx, dc in PEERS[1:]:
        pl.semaphore_signal(barrier, inc=1, device_id=device(dx, 0, 0, dc), device_id_type=MESH)

    def greet(k, carry):
        pl.semaphore_signal(barrier, inc=1, device_id=device(0, lax.div(k, NZ), lax.rem(k, NZ)), device_id_type=MESH)
        return carry

    lax.fori_loop(1, NT, greet, 0)

    areas = (pl.ds(YZ_COLS, D - YZ_COLS), pl.ds(0, YZ_COLS))

    def own_copy(number):
        if number < 4:
            area, which = areas[number // 2], number % 2
            return pltpu.make_async_copy(
                (gate_ref, up_ref)[which].at[area], weights.at[which, area], w_own.at[number]
            )
        return pltpu.make_async_copy(down_ref, downs, w_own.at[number])

    for number in range(5):
        own_copy(number).start()

    nodes = []

    def message(way, size, src, dst, deps=(), act=None, cost=0.04, bundle=None, sender=0, mark=None):
        nodes.append(Node(deps, cost, act, way, size, src, dst, bundle=bundle, sender=sender, mark=mark))
        return len(nodes) - 1

    def task(act, deps, cost, pause=0.0):
        nodes.append(Node(deps, cost, act, pause=pause))
        return len(nodes) - 1

    def sign(row, column):
        common = row & column
        common = common ^ (common >> 4)
        common = common ^ (common >> 2)
        common = common ^ (common >> 1)
        return (1 - 2 * (common & 1)).astype(F32)

    def iotas(rows, columns):
        shape = (rows, columns)
        return lax.broadcasted_iota(jnp.int32, shape, 0), lax.broadcasted_iota(jnp.int32, shape, 1)

    def lands(dx, dc):
        return PEERS.index((-dx % 4, dc))

    def peer_way(number):
        dx, dc = PEERS[number]
        return (-1 if dx == 3 else dx, 0, 0, dc)

    def tables():
        row, column = iotas(TOK, TOK)
        earlier = (row < column).astype(F32).astype(BF16)
        slots = iotas(CAP, TOK)[0].astype(F32)
        first, second = routes_ref[0:1, :], routes_ref[1:2, :]
        gain_1, gain_2 = gains_ref[0:1, :].astype(F32), gains_ref[1:2, :].astype(F32)
        for number, (dx, dc) in enumerate(PEERS):
            expert = device(dx, 0, 0, dc)[0]
            is_1, is_2 = (first == expert).astype(F32), (second == expert).astype(F32)
            named = is_1 + is_2
            place = jnp.dot(
                jnp.broadcast_to(named, (16, TOK)).astype(BF16), earlier, preferred_element_type=F32
            )[0:1]
            hit = jnp.where(slots == place, 1.0, 0.0) * named
            area = slice(number * CAP, (number + 1) * CAP)
            pick[area, :] = hit.astype(BF16)
            blend[area, :] = (hit * ((is_1 * gain_1 + is_2 * gain_2) * (1.0 / 16.0))).astype(BF16)

    def slice_rows():
        columns = pl.ds(pl.multiple_of(own_t * 128, 128), 128)
        sliced[...] = jnp.dot(pick[...], tok_ref[:, columns], preferred_element_type=F32).astype(BF16)

    def chunk_rows(k):
        columns = tok_ref[:, YZ_COLS + 512 * k : YZ_COLS + 512 * (k + 1)]
        rows = jnp.dot(pick[...], columns, preferred_element_type=F32).astype(BF16)
        wide[k, 0:CAP, :] = rows[0:CAP]
        for number in range(1, 8):
            chunked[k, number] = rows[number * CAP : (number + 1) * CAP]

    def near_rows():
        for t in range(NT):
            columns = tok_ref[:, t * 128 : (t + 1) * 128]
            rows = jnp.dot(pick[0 : 2 * CAP, :], columns, preferred_element_type=F32).astype(BF16)
            tiles[t, 0:CAP, :] = rows[0:CAP]
            near[t] = rows[CAP : 2 * CAP]

    tables()
    slice_rows()
    chunk_tasks = [task(lambda k=k: chunk_rows(k), [], 0.25) for k in range(4)]
    near_task = task(near_rows, chunk_tasks, 0.5)

    slices, chunk_nodes = [], []
    for number in (2, 3, 4, 5, 6, 7):
        slices.append(message(
            peer_way(number), 16384,
            lambda number=number: sliced.at[pl.ds(number * CAP, CAP)],
            lambda number=number: tiles.at[own_t, pl.ds(lands(*PEERS[number]) * CAP, CAP)],
            bundle="slices",
        ))
    for k in range(4):
        chunk_nodes.append([
            message(
                peer_way(number), 65536,
                lambda k=k, number=number: chunked.at[k, number],
                lambda k=k, number=number: wide.at[k, pl.ds(lands(*PEERS[number]) * CAP, CAP)],
                [chunk_tasks[k]] + (chunk_nodes[k - 2] if k > 1 else []), bundle=("chunk", k),
            )
            for number in (2, 3, 4, 5, 6, 7, 1)
        ])
    near_node = message(
        (0, 0, 0, 1), 524288, lambda: near, lambda: tiles.at[pl.ds(0, NT), pl.ds(CAP, CAP)], [near_task]
    )
    group_nodes = [list(slices), [], [], []]
    base = len(nodes)
    for index, ((dy, dz), (sy, sz), (low, count), deps) in enumerate(tree(*GATHER)):
        def ref(sy=sy, sz=sz, low=low, count=count):
            return tiles.at[slot(sy, sz), pl.ds(low, count)]

        number = message(
            (0, dy, dz), count * 256, ref, ref, [base + d for d in deps] if deps else slices,
            sender=1, mark=("tree", index),
        )
        group_nodes[(sy - dy) % 4].append(number)

    def fold_signs():
        fold[...] = sign(*iotas(HID, HID)).astype(BF16)

    def mix_signs(low):
        row, column = iotas(2 * CAP, 2 * HID)
        row = row + low
        mix[low : low + 2 * CAP, :] = jnp.where(
            (row & 15) == (column & 15), sign(row >> 4, column >> 4), 0.0
        ).astype(BF16)

    fold_task = task(fold_signs, [near_task], 0.1)
    mix_tasks = [task(lambda n=n: mix_signs(n * 2 * CAP), [fold_task], 0.05) for n in range(4)]

    def weights_wait(low):
        own_copy(low).wait()
        own_copy(low + 1).wait()

    wide_weights = task(lambda: weights_wait(0), [near_task], 0.02)
    tile_weights = task(lambda: weights_wait(2), [wide_weights], 0.02)

    started = []

    def accumulate(rows, low, count):
        fresh = not started
        started.append(low)
        for which in range(2):
            term = jnp.dot(rows, weights[which, pl.ds(low, count), :], preferred_element_type=F32)
            acc[which] = term if fresh else acc[which] + term

    def group_dot(group):
        base_y = lax.rem(y + group, NY)
        rows = jnp.concatenate([tiles[base_y * NZ + j] for j in range(NZ)], axis=1)
        accumulate(rows, base_y * 1024, 1024)

    def chunk_dot(k):
        accumulate(wide[k], YZ_COLS + 512 * k, 512)

    def block(group):
        return pl.ds(pl.multiple_of(lax.rem(y + group, NY) * TOK, TOK), TOK)

    def hide():
        for group in (2, 1, 3, 0):
            gate, up = acc[0, block(group), :], acc[1, block(group), :]
            hidden = (gate / (1.0 + jnp.exp(-gate)) * up).astype(BF16)
            sent_rows[block(group), :] = jnp.dot(hidden, fold[...], preferred_element_type=F32).astype(BF16)
            start_block(sent_rows, got_rows, 0, group)

    def piece(t):
        return pl.ds(pl.multiple_of(t * 16, 16), 16)

    def start_block(src, dst, turn, group):
        for dz in (4, 3, -3, 2, -2, 1, -1, 0):
            other = slot(group, dz)
            if group or dz:
                pltpu.make_async_remote_copy(
                    src_ref=src.at[piece(other)], dst_ref=dst.at[piece(own_t)],
                    send_sem=b_send.at[turn], recv_sem=b_recv.at[turn],
                    device_id=(own_e, other), device_id_type=MESH,
                ).start()
            else:
                dst[piece(own_t), :] = src[piece(own_t), :]

    def all_of(ref, turn):
        area = ref.at[pl.ds(0, (NT - 1) * 16)]
        return pltpu.make_async_remote_copy(
            src_ref=area, dst_ref=area, send_sem=b_send.at[turn], recv_sem=b_recv.at[turn],
            device_id=(own_e, slot(0, 1)), device_id_type=MESH,
        )

    def rotate():
        all_of(got_rows, 0).wait_recv()
        for group in (2, 1, 3, 0):
            values = jnp.dot(mix[block(group), :], got_rows[...], preferred_element_type=F32)
            back_rows[block(group), :] = (values * (1.0 / math.sqrt(NT * HID))).astype(BF16)
            start_block(back_rows, turned, 1, group)

    dots = [task(lambda k=k: chunk_dot(k), chunk_nodes[k] + [chunk_tasks[k], wide_weights], 0.5) for k in range(4)]
    for group in (0, 1, 3, 2):
        dots.append(task(
            lambda group=group: group_dot(group),
            group_nodes[group] + [tile_weights, near_node, near_task], 0.9,
        ))
    gone = task(hide, dots + [fold_task], 1.6)
    back = task(rotate, [gone] + mix_tasks, 1.5, B_PAUSE)
    come = task(lambda: all_of(turned, 1).wait_recv(), [back], 0.1, B_PAUSE)

    down_task = task(lambda: own_copy(4).wait(), [tile_weights], 0.02)

    def down_dot(group):
        base_y = lax.rem(y + group, NY)
        for side in range(2):
            columns = pl.ds(pl.multiple_of(base_y * 1536 + side * 768, 128), 768)
            values = jnp.dot(turned[...], downs[:, columns], preferred_element_type=F32).astype(BF16)
            for pair in range(2):
                q = 2 * side + pair
                low = 384 * pair
                part[base_y * NZ + 2 * q] = values[:, low : low + 128]
                part[base_y * NZ + 2 * q + 1] = values[:, low + 256 : low + 384]
                for number in range(8):
                    into = cross_in if number == 0 else cross
                    into[group, number, q] = values[number * CAP : (number + 1) * CAP, low + 128 : low + 256]

    group_task, cross_nodes = {}, {}
    for group in (2, 1, 3, 0):
        group_task[group] = task(lambda group=group: down_dot(group), [come, down_task], 0.8)
        cross_nodes[group] = [
            message(
                peer_way(n), 65536, lambda group=group, n=n: cross.at[group, n],
                lambda group=group, n=n: cross_in.at[group, lands(*PEERS[n])],
                [group_task[group]], bundle=("cross", group), sender=2,
            )
            for n in (2, 3, 4, 5, 6, 7, 1)
        ]

    def blended(rows):
        return lax.dot_general(rows, blend[...], (((0,), (0,)), ((), ())), preferred_element_type=F32)

    packed = {}
    for group in (2, 1, 3, 0):
        def pack(group=group):
            for q in range(4):
                sums = blended(cross_in[group, 0:8, q].reshape(8 * CAP, 128)).astype(BF16)
                over[group, 2 * q] = sums[0:CAP]
                over[group, 2 * q + 1] = sums[CAP : 2 * CAP]

        packed[group] = task(pack, cross_nodes[group] + [group_task[group]], 0.4)

    over_nodes = [
        message(
            (0, -1 if group == 3 else group, 0), 131072, lambda group=group: over.at[group],
            lambda group=group: over_in.at[group - 1], [packed[group]], sender=2,
        )
        for group in (2, 1, 3)
    ]

    def add_over():
        for n in range(NZ):
            sums = over[0, n].astype(F32)
            for index in range(3):
                sums = sums + over_in[index, n].astype(F32)
            over[0, n] = sums.astype(BF16)

    over_task = task(add_over, over_nodes + [packed[0]], 0.3)
    ends = [
        message(
            (0, 0, dz), 16384, lambda dz=dz: over.at[0, lax.rem(z + dz + NZ, NZ)],
            lambda dz=dz: over_last.at[dz % NZ - 1], [over_task], bundle="over", sender=2,
        )
        for dz in (4, 3, -3, 2, -2, 1, -1)
    ]

    total, base = 0, len(nodes)
    reduction = tree(*REDUCE)
    roots = {False: [group_task[0]], True: [group_task[0]]}
    for number, ((dy, dz), (sy, sz), (low, count), deps) in enumerate(reduction):
        def src(sy=sy, sz=sz, dy=dy, dz=dz, low=low, count=count):
            return part.at[slot(sy - dy, sz - dz), pl.ds(low, count)]

        def dst(total=total, count=count):
            return part_in.at[pl.ds(total, count)]

        def act(sy=sy, sz=sz, low=low, count=count, total=total):
            here = slot(sy, sz)
            part[here, low : low + count, :] = part[here, low : low + count, :] + part_in[total : total + count, :]

        children = [base + n for n, other in enumerate(reduction) if number in other[3]]
        if not deps:
            roots[low >= REDUCE[1][0]].append(base + number)
        needs = [group_task[(sy - dy) % 4], group_task[sy % 4]]
        message((0, -dy, -dz), count * 256, src, dst, children + needs, act, count / 4000, sender=3, mark=("tree", number))
        total += count
    lasts = [
        message(
            peer_way(n), 16384, lambda n=n: part.at[own_t, pl.ds(n * CAP, CAP)],
            lambda n=n: last_in.at[pl.ds(lands(*PEERS[n]) * CAP, CAP)], roots[n > 3], bundle="last", sender=2,
        )
        for n in (2, 3, 4, 5, 6, 7, 1)
    ]

    def store():
        last_in[0:CAP, :] = part[own_t, 0:CAP, :]
        summed = blended(last_in[...])
        odd = lax.rem(own_t, 2)
        out_ref[pl.ds(pl.multiple_of(odd * CAP, CAP), TOK), :] = summed.astype(BF16)
        extra = over[0, z].astype(F32)
        for index in range(NZ - 1):
            extra = extra + over_last[index].astype(F32)
        out_ref[pl.ds(pl.multiple_of((1 - odd) * TOK, CAP), CAP), :] = extra.astype(BF16)

    task(store, lasts + ends, 0.2)

    marks = sorted({str(node.mark) for node in nodes if node.way and node.mark})
    marks += [str(number) for number, node in enumerate(nodes) if node.way and not node.mark]

    def copy_of(number, src=None, dst=None):
        node = nodes[number]
        return pltpu.make_async_remote_copy(
            src_ref=src or node.src(), dst_ref=dst or node.dst(),
            send_sem=sends.at[node.sender], recv_sem=recvs.at[marks.index(str(node.mark or number))],
            device_id=device(*node.way), device_id_type=MESH,
        )

    def rows_of(chosen):
        return part_in.at[pl.ds(0, sum(node.size for node in chosen) // 256)]

    pl.semaphore_wait(barrier, NT - 1 + 7)
    taken = {}
    for kind, number in steps_of(nodes):
        node = nodes[number]
        if kind == "send":
            copy_of(number).start()
            continue
        if kind == "take" and node.bundle:
            members = [other for other in nodes if other.bundle == node.bundle]
            taken[node.bundle] = taken.get(node.bundle, 0) + 1
            if taken[node.bundle] == len(members):
                area = rows_of(members)
                copy_of(number, area, area).wait_recv()
        elif kind == "take":
            copy_of(number).wait_recv()
        if node.act:
            node.act()

    for sender in range(4):
        chosen = [number for number, node in enumerate(nodes) if node.way and node.sender == sender]
        area = rows_of([nodes[number] for number in chosen])
        copy_of(chosen[0], area, area).wait_send()
    for turn in range(2):
        all_of(back_rows, turn).wait_send()


def shards(tokens, routes, gate_num, gate_weight, up_weight, down_weight):
    vmem, anywhere = pl.BlockSpec(memory_space=pltpu.VMEM), pl.BlockSpec(memory_space=pl.ANY)
    dma = pltpu.SemaphoreType.DMA
    return pl.pallas_call(
        kernel,
        out_shape=jax.ShapeDtypeStruct((192, TOK), BF16),
        in_specs=[vmem, vmem, vmem, anywhere, anywhere, anywhere],
        out_specs=vmem,
        scratch_shapes=[
            pltpu.VMEM((2, D, HID), BF16),
            pltpu.VMEM((HID, D), BF16),
            pltpu.VMEM((NT, 8 * CAP, 128), BF16),
            pltpu.VMEM((4, 8 * CAP, 512), BF16),
            pltpu.VMEM((8 * CAP, 128), BF16),
            pltpu.VMEM((4, 8, CAP, 512), BF16),
            pltpu.VMEM((NT, CAP, 128), BF16),
            pltpu.VMEM((2, 8 * CAP, HID), F32),
            pltpu.VMEM((8 * CAP, TOK), BF16),
            pltpu.VMEM((8 * CAP, TOK), BF16),
            pltpu.VMEM((HID, HID), BF16),
            pltpu.VMEM((2 * HID, 2 * HID), BF16),
            pltpu.VMEM((8 * CAP, HID), BF16),
            pltpu.VMEM((8 * CAP, HID), BF16),
            pltpu.VMEM((8 * CAP, HID), BF16),
            pltpu.VMEM((8 * CAP, HID), BF16),
            pltpu.VMEM((NT, 8 * CAP, 128), BF16),
            pltpu.VMEM((15872, 128), BF16),
            pltpu.VMEM((4, 8, 4, CAP, 128), BF16),
            pltpu.VMEM((4, 8, 4, CAP, 128), BF16),
            pltpu.VMEM((4, NZ, CAP, 128), BF16),
            pltpu.VMEM((3, NZ, CAP, 128), BF16),
            pltpu.VMEM((NZ - 1, CAP, 128), BF16),
            pltpu.VMEM((8 * CAP, 128), BF16),
            dma((4,)), dma((91,)), dma((2,)), dma((2,)), dma((5,)),
        ],
        compiler_params=pltpu.CompilerParams(
            collective_id=0, has_side_effects=True, vmem_limit_bytes=60 * 2**20
        ),
        cost_estimate=pl.CostEstimate(flops=10**10, bytes_accessed=2 * 10**7, transcendentals=2**18),
        name="moe_layer",
    )(routes.T, gate_num.T, tokens, gate_weight[0], up_weight[0], down_weight[0]).T


def solution(mesh):
    placed = (
        P("expert", None),
        P("expert", None),
        P("expert", None),
        P("expert", None, "tensor"),
        P("expert", None, "tensor"),
        P("expert", "tensor", None),
    )
    return jax.shard_map(
        shards, mesh=mesh, in_specs=placed, out_specs=P("expert", "tensor"), check_vma=False
    )
```

```python
import math

import jax
import jax.numpy as jnp
from jax import lax
from jax.experimental import pallas as pl
from jax.experimental.pallas import tpu as pltpu
from jax.sharding import PartitionSpec as P

NX, NY, NZ, NT = 4, 4, 8, 32
CAP, TOK, D, HID = 64, 128, 6144, 256
YZ_COLS = NT * 128
MESH = pl.DeviceIdType.MESH
BF16, F32 = jnp.bfloat16, jnp.float32

PEERS = tuple((dx, dc) for dx in (0, 2, 1, 3) for dc in (0, 1))
GATHER = ((128, 256), (384, 128))
REDUCE = ((0, 256), (256, 256))
LATENCY, B_PAUSE = 1.6, 6.0


class Node:
    def __init__(self, deps, cost, act=None, way=None, size=0, src=None, dst=None, pause=0.0, bundle=None, sender=None, mark=None):
        self.deps, self.cost, self.act, self.pause = list(deps), cost, act, pause
        self.way, self.size, self.src, self.dst, self.bundle, self.sender = way, size, src, dst, bundle, sender
        self.mark = mark or bundle


def steps_of(nodes):
    done, sent, steps, now, link, due = set(), set(), [], 0.0, {}, {}

    def occupy(way, size):
        end = now
        for axis, hops in enumerate(way[:3]):
            both = abs(hops) * 2 == (NX, NY, NZ)[axis]
            for sign in (1, -1) if both else (1,) if hops > 0 else (-1,):
                if hops:
                    key = (axis, sign)
                    link[key] = max(now, link.get(key, 0.0)) + size * 2 / 1e5 * abs(hops) / (2 if both else 1)
                    end = max(end, link[key])
        return end + 0.6 * max(0, sum(abs(hops) for hops in way[:3]) - 1)

    def send_ready():
        for i, node in enumerate(nodes):
            if i not in due and all(d in done for d in node.deps):
                if node.way:
                    due[i] = occupy(node.way, node.size) + LATENCY
                    sent.add(i)
                    steps.append(("send", i))
                else:
                    due[i] = now + node.pause

    send_ready()
    while len(done) < len(nodes):
        ready = [(due[i], i) for i in due if i not in done]
        arrived = [r for r in ready if r[1] in sent and r[0] <= now]
        tasks = [r[1] for r in ready if r[1] not in sent and r[0] <= now]
        if arrived:
            pick = min(arrived)[1]
        elif tasks:
            pick = min(tasks)
        else:
            now, pick = min(ready)
        steps.append(("take" if nodes[pick].way else "task", pick))
        done.add(pick)
        now += nodes[pick].cost
        send_ready()
    return steps


def halves(rows):
    low, count = rows
    return (low, count // 2), (low + count // 2, count // 2)


def tree(p_rows, q_rows):
    found = []

    def add(way, slot, rows, deps):
        found.append((way, slot, rows, list(deps)))
        return len(found) - 1

    def ring(offset_y, rows, deps, arrived):
        for way, half in ((1, 0), (-1, 1)):
            before = deps
            for step in range(4):
                part = rows if step < 3 else halves(rows)[half]
                before = [add((0, way), (offset_y, -way * step), part, before)]
                arrived.setdefault(way * 4 if step == 3 else -way * (step + 1), []).extend(before)

    arrived = {}
    ring(0, p_rows, [], arrived)
    arrived = {0: [], 4: arrived.pop(4) + arrived.pop(-4), **arrived}
    for offset_z in (4, 3, -3, 2, -2, 1, -1, 0):
        up = add((1, 0), (0, offset_z), p_rows, arrived[offset_z])
        down = add((-1, 0), (0, offset_z), p_rows, arrived[offset_z])
        add((1, 0), (-1, offset_z), halves(p_rows)[0], [up])
        add((-1, 0), (1, offset_z), halves(p_rows)[1], [down])
    up = add((1, 0), (0, 0), q_rows, [])
    down = add((-1, 0), (0, 0), q_rows, [])
    far = [add((1, 0), (-1, 0), halves(q_rows)[0], [up]), add((-1, 0), (1, 0), halves(q_rows)[1], [down])]
    for offset_y, deps in ((0, []), (-1, [up]), (1, [down]), (2, far)):
        ring(offset_y, q_rows, deps, {})
    return found


def kernel(
    routes_ref, gains_ref, tok_ref, gate_ref, up_ref, down_ref, out_ref,
    weights, downs, tiles, wide, sliced, chunked, near, acc, pick, blend, fold, mix,
    sent_rows, got_rows, back_rows, turned, part, part_in, cross, cross_in, over, over_in, over_last, last_in,
    sends, recvs, b_send, b_recv, w_own,
):
    own_e, own_t = lax.axis_index("expert"), lax.axis_index("tensor")
    x, c = lax.div(own_e, 2), lax.rem(own_e, 2)
    y, z = lax.div(own_t, NZ), lax.rem(own_t, NZ)

    def slot(dy, dz):
        return lax.rem(y + dy + NY, NY) * NZ + lax.rem(z + dz + NZ, NZ)

    def device(dx, dy, dz, dc=0):
        return (lax.rem(x + dx + NX, NX) * 2 + (1 - c if dc else c), slot(dy, dz))

    barrier = pltpu.get_barrier_semaphore()
    for dx, dc in PEERS[1:]:
        pl.semaphore_signal(barrier, inc=1, device_id=device(dx, 0, 0, dc), device_id_type=MESH)

    for dz in (4, 3, -3, 2, -2, 1, -1, 0):
        for dy in (2, 1, -1, 0):
            if dy or dz:
                pl.semaphore_signal(barrier, inc=1, device_id=device(0, dy, dz), device_id_type=MESH)

    areas = (pl.ds(YZ_COLS, D - YZ_COLS), pl.ds(0, YZ_COLS))

    def own_copy(number):
        if number < 4:
            area, which = areas[number // 2], number % 2
            return pltpu.make_async_copy(
                (gate_ref, up_ref)[which].at[area], weights.at[which, area], w_own.at[number]
            )
        return pltpu.make_async_copy(down_ref, downs, w_own.at[number])

    for number in range(5):
        own_copy(number).start()

    nodes = []

    def message(way, size, src, dst, deps=(), act=None, cost=0.04, bundle=None, sender=0, mark=None):
        nodes.append(Node(deps, cost, act, way, size, src, dst, bundle=bundle, sender=sender, mark=mark))
        return len(nodes) - 1

    def task(act, deps, cost, pause=0.0):
        nodes.append(Node(deps, cost, act, pause=pause))
        return len(nodes) - 1

    def sign(row, column):
        common = row & column
        common = common ^ (common >> 4)
        common = common ^ (common >> 2)
        common = common ^ (common >> 1)
        return (1 - 2 * (common & 1)).astype(F32)

    def iotas(rows, columns):
        shape = (rows, columns)
        return lax.broadcasted_iota(jnp.int32, shape, 0), lax.broadcasted_iota(jnp.int32, shape, 1)

    def lands(dx, dc):
        return PEERS.index((-dx % 4, dc))

    def peer_way(number):
        dx, dc = PEERS[number]
        return (-1 if dx == 3 else dx, 0, 0, dc)

    def tables():
        row, column = iotas(TOK, TOK)
        earlier = (row < column).astype(F32).astype(BF16)
        slots = iotas(CAP, TOK)[0].astype(F32)
        first, second = routes_ref[0:1, :], routes_ref[1:2, :]
        gain_1, gain_2 = gains_ref[0:1, :].astype(F32), gains_ref[1:2, :].astype(F32)
        for number, (dx, dc) in enumerate(PEERS):
            expert = device(dx, 0, 0, dc)[0]
            is_1, is_2 = (first == expert).astype(F32), (second == expert).astype(F32)
            named = is_1 + is_2
            place = jnp.dot(
                jnp.broadcast_to(named, (16, TOK)).astype(BF16), earlier, preferred_element_type=F32
            )[0:1]
            hit = jnp.where(slots == place, 1.0, 0.0) * named
            area = slice(number * CAP, (number + 1) * CAP)
            pick[area, :] = hit.astype(BF16)
            blend[area, :] = (hit * ((is_1 * gain_1 + is_2 * gain_2) * (1.0 / 16.0))).astype(BF16)

    def slice_rows():
        columns = pl.ds(pl.multiple_of(own_t * 128, 128), 128)
        sliced[...] = jnp.dot(pick[...], tok_ref[:, columns], preferred_element_type=F32).astype(BF16)

    def chunk_rows(k):
        columns = tok_ref[:, YZ_COLS + 512 * k : YZ_COLS + 512 * (k + 1)]
        rows = jnp.dot(pick[...], columns, preferred_element_type=F32).astype(BF16)
        wide[k, 0:CAP, :] = rows[0:CAP]
        for number in range(1, 8):
            chunked[k, number] = rows[number * CAP : (number + 1) * CAP]

    def near_rows():
        for t in range(NT):
            columns = tok_ref[:, t * 128 : (t + 1) * 128]
            rows = jnp.dot(pick[0 : 2 * CAP, :], columns, preferred_element_type=F32).astype(BF16)
            tiles[t, 0:CAP, :] = rows[0:CAP]
            near[t] = rows[CAP : 2 * CAP]

    tables()
    slice_rows()
    chunk_tasks = [task(lambda k=k: chunk_rows(k), [], 0.25) for k in range(4)]
    near_task = task(near_rows, chunk_tasks, 0.5)

    slices, chunk_nodes = [], []
    for number in (2, 3, 4, 5, 6, 7):
        slices.append(message(
            peer_way(number), 16384,
            lambda number=number: sliced.at[pl.ds(number * CAP, CAP)],
            lambda number=number: tiles.at[own_t, pl.ds(lands(*PEERS[number]) * CAP, CAP)],
            bundle="slices",
        ))
    for k in range(4):
        chunk_nodes.append([
            message(
                peer_way(number), 65536,
                lambda k=k, number=number: chunked.at[k, number],
                lambda k=k, number=number: wide.at[k, pl.ds(lands(*PEERS[number]) * CAP, CAP)],
                [chunk_tasks[k]] + (chunk_nodes[k - 2] if k > 1 else []), bundle=("chunk", k),
            )
            for number in (2, 3, 4, 5, 6, 7, 1)
        ])
    near_node = message(
        (0, 0, 0, 1), 524288, lambda: near, lambda: tiles.at[pl.ds(0, NT), pl.ds(CAP, CAP)], [near_task]
    )
    group_nodes = [list(slices), [], [], []]
    base = len(nodes)
    for index, ((dy, dz), (sy, sz), (low, count), deps) in enumerate(tree(*GATHER)):
        def ref(sy=sy, sz=sz, low=low, count=count):
            return tiles.at[slot(sy, sz), pl.ds(low, count)]

        number = message(
            (0, dy, dz), count * 256, ref, ref, [base + d for d in deps] if deps else slices,
            sender=1, mark=("tree", index),
        )
        group_nodes[(sy - dy) % 4].append(number)

    def fold_signs():
        fold[...] = sign(*iotas(HID, HID)).astype(BF16)

    def mix_signs(low):
        row, column = iotas(2 * CAP, 2 * HID)
        row = row + low
        mix[low : low + 2 * CAP, :] = jnp.where(
            (row & 15) == (column & 15), sign(row >> 4, column >> 4), 0.0
        ).astype(BF16)

    fold_task = task(fold_signs, [near_task], 0.1)
    mix_tasks = [task(lambda n=n: mix_signs(n * 2 * CAP), [fold_task], 0.05) for n in range(4)]

    def weights_wait(low):
        own_copy(low).wait()
        own_copy(low + 1).wait()

    wide_weights = task(lambda: weights_wait(0), [near_task], 0.02)
    tile_weights = task(lambda: weights_wait(2), [wide_weights], 0.02)

    started = []

    def accumulate(rows, low, count):
        fresh = not started
        started.append(low)
        for which in range(2):
            term = jnp.dot(rows, weights[which, pl.ds(low, count), :], preferred_element_type=F32)
            acc[which] = term if fresh else acc[which] + term

    def group_dot(group):
        base_y = lax.rem(y + group, NY)
        rows = jnp.concatenate([tiles[base_y * NZ + j] for j in range(NZ)], axis=1)
        accumulate(rows, base_y * 1024, 1024)

    def chunk_dot(k):
        accumulate(wide[k], YZ_COLS + 512 * k, 512)

    def block(group):
        return pl.ds(pl.multiple_of(lax.rem(y + group, NY) * TOK, TOK), TOK)

    def hide():
        for group in (2, 1, 3, 0):
            gate, up = acc[0, block(group), :], acc[1, block(group), :]
            hidden = (gate / (1.0 + jnp.exp(-gate)) * up).astype(BF16)
            sent_rows[block(group), :] = jnp.dot(hidden, fold[...], preferred_element_type=F32).astype(BF16)
            start_block(sent_rows, got_rows, 0, group)

    def piece(t):
        return pl.ds(pl.multiple_of(t * 16, 16), 16)

    def start_block(src, dst, turn, group):
        for dz in (4, 3, -3, 2, -2, 1, -1, 0):
            other = slot(group, dz)
            if group or dz:
                pltpu.make_async_remote_copy(
                    src_ref=src.at[piece(other)], dst_ref=dst.at[piece(own_t)],
                    send_sem=b_send.at[turn], recv_sem=b_recv.at[turn],
                    device_id=(own_e, other), device_id_type=MESH,
                ).start()
            else:
                dst[piece(own_t), :] = src[piece(own_t), :]

    def all_of(ref, turn):
        area = ref.at[pl.ds(0, (NT - 1) * 16)]
        return pltpu.make_async_remote_copy(
            src_ref=area, dst_ref=area, send_sem=b_send.at[turn], recv_sem=b_recv.at[turn],
            device_id=(own_e, slot(0, 1)), device_id_type=MESH,
        )

    def rotate():
        all_of(got_rows, 0).wait_recv()
        for group in (2, 1, 3, 0):
            values = jnp.dot(mix[block(group), :], got_rows[...], preferred_element_type=F32)
            back_rows[block(group), :] = (values * (1.0 / math.sqrt(NT * HID))).astype(BF16)
            start_block(back_rows, turned, 1, group)

    dots = [task(lambda k=k: chunk_dot(k), chunk_nodes[k] + [chunk_tasks[k], wide_weights], 0.5) for k in range(4)]
    for group in (0, 1, 3, 2):
        dots.append(task(
            lambda group=group: group_dot(group),
            group_nodes[group] + [tile_weights, near_node, near_task], 0.9,
        ))
    gone = task(hide, dots + [fold_task], 1.6)
    back = task(rotate, [gone] + mix_tasks, 1.5, B_PAUSE)
    come = task(lambda: all_of(turned, 1).wait_recv(), [back], 0.1, B_PAUSE)

    down_task = task(lambda: own_copy(4).wait(), [tile_weights], 0.02)

    def down_dot(group):
        base_y = lax.rem(y + group, NY)
        for side in range(2):
            columns = pl.ds(pl.multiple_of(base_y * 1536 + side * 768, 128), 768)
            values = jnp.dot(turned[...], downs[:, columns], preferred_element_type=F32).astype(BF16)
            for pair in range(2):
                q = 2 * side + pair
                low = 384 * pair
                part[base_y * NZ + 2 * q] = values[:, low : low + 128]
                part[base_y * NZ + 2 * q + 1] = values[:, low + 256 : low + 384]
                for number in range(8):
                    into = cross_in if number == 0 else cross
                    into[group, number, q] = values[number * CAP : (number + 1) * CAP, low + 128 : low + 256]

    group_task, cross_nodes = {}, {}
    for group in (2, 1, 3, 0):
        group_task[group] = task(lambda group=group: down_dot(group), [come, down_task], 0.8)
        cross_nodes[group] = [
            message(
                peer_way(n), 65536, lambda group=group, n=n: cross.at[group, n],
                lambda group=group, n=n: cross_in.at[group, lands(*PEERS[n])],
                [group_task[group]], bundle=("cross", group), sender=2,
            )
            for n in (2, 3, 4, 5, 6, 7, 1)
        ]

    def blended(rows):
        return lax.dot_general(rows, blend[...], (((0,), (0,)), ((), ())), preferred_element_type=F32)

    packed = {}
    for group in (2, 1, 3, 0):
        def pack(group=group):
            for q in range(4):
                sums = blended(cross_in[group, 0:8, q].reshape(8 * CAP, 128)).astype(BF16)
                over[group, 2 * q] = sums[0:CAP]
                over[group, 2 * q + 1] = sums[CAP : 2 * CAP]

        packed[group] = task(pack, cross_nodes[group] + [group_task[group]], 0.4)

    over_nodes = [
        message(
            (0, -1 if group == 3 else group, 0), 131072, lambda group=group: over.at[group],
            lambda group=group: over_in.at[group - 1], [packed[group]], sender=2,
        )
        for group in (2, 1, 3)
    ]

    def add_over():
        for n in range(NZ):
            sums = over[0, n].astype(F32)
            for index in range(3):
                sums = sums + over_in[index, n].astype(F32)
            over[0, n] = sums.astype(BF16)

    over_task = task(add_over, over_nodes + [packed[0]], 0.3)
    ends = [
        message(
            (0, 0, dz), 16384, lambda dz=dz: over.at[0, lax.rem(z + dz + NZ, NZ)],
            lambda dz=dz: over_last.at[dz % NZ - 1], [over_task], bundle="over", sender=2,
        )
        for dz in (4, 3, -3, 2, -2, 1, -1)
    ]

    total, base = 0, len(nodes)
    reduction = tree(*REDUCE)
    roots = {False: [group_task[0]], True: [group_task[0]]}
    for number, ((dy, dz), (sy, sz), (low, count), deps) in enumerate(reduction):
        def src(sy=sy, sz=sz, dy=dy, dz=dz, low=low, count=count):
            return part.at[slot(sy - dy, sz - dz), pl.ds(low, count)]

        def dst(total=total, count=count):
            return part_in.at[pl.ds(total, count)]

        def act(sy=sy, sz=sz, low=low, count=count, total=total):
            here = slot(sy, sz)
            part[here, low : low + count, :] = part[here, low : low + count, :] + part_in[total : total + count, :]

        children = [base + n for n, other in enumerate(reduction) if number in other[3]]
        if not deps:
            roots[low >= REDUCE[1][0]].append(base + number)
        needs = [group_task[(sy - dy) % 4], group_task[sy % 4]]
        message((0, -dy, -dz), count * 256, src, dst, children + needs, act, count / 4000, sender=3, mark=("tree", number))
        total += count
    lasts = [
        message(
            peer_way(n), 16384, lambda n=n: part.at[own_t, pl.ds(n * CAP, CAP)],
            lambda n=n: last_in.at[pl.ds(lands(*PEERS[n]) * CAP, CAP)], roots[n > 3], bundle="last", sender=2,
        )
        for n in (2, 3, 4, 5, 6, 7, 1)
    ]

    def store():
        last_in[0:CAP, :] = part[own_t, 0:CAP, :]
        summed = blended(last_in[...])
        odd = lax.rem(own_t, 2)
        out_ref[pl.ds(pl.multiple_of(odd * CAP, CAP), TOK), :] = summed.astype(BF16)
        extra = over[0, z].astype(F32)
        for index in range(NZ - 1):
            extra = extra + over_last[index].astype(F32)
        out_ref[pl.ds(pl.multiple_of((1 - odd) * TOK, CAP), CAP), :] = extra.astype(BF16)

    task(store, lasts + ends, 0.2)

    marks = sorted({str(node.mark) for node in nodes if node.way and node.mark})
    marks += [str(number) for number, node in enumerate(nodes) if node.way and not node.mark]

    def copy_of(number, src=None, dst=None):
        node = nodes[number]
        return pltpu.make_async_remote_copy(
            src_ref=src or node.src(), dst_ref=dst or node.dst(),
            send_sem=sends.at[node.sender], recv_sem=recvs.at[marks.index(str(node.mark or number))],
            device_id=device(*node.way), device_id_type=MESH,
        )

    def rows_of(chosen):
        return part_in.at[pl.ds(0, sum(node.size for node in chosen) // 256)]

    pl.semaphore_wait(barrier, NT - 1 + 7)
    taken = {}
    for kind, number in steps_of(nodes):
        node = nodes[number]
        if kind == "send":
            copy_of(number).start()
            continue
        if kind == "take" and node.bundle:
            members = [other for other in nodes if other.bundle == node.bundle]
            taken[node.bundle] = taken.get(node.bundle, 0) + 1
            if taken[node.bundle] == len(members):
                area = rows_of(members)
                copy_of(number, area, area).wait_recv()
        elif kind == "take":
            copy_of(number).wait_recv()
        if node.act:
            node.act()

    for sender in range(4):
        chosen = [number for number, node in enumerate(nodes) if node.way and node.sender == sender]
        area = rows_of([nodes[number] for number in chosen])
        copy_of(chosen[0], area, area).wait_send()
    for turn in range(2):
        all_of(back_rows, turn).wait_send()


def shards(tokens, routes, gate_num, gate_weight, up_weight, down_weight):
    vmem, anywhere = pl.BlockSpec(memory_space=pltpu.VMEM), pl.BlockSpec(memory_space=pl.ANY)
    dma = pltpu.SemaphoreType.DMA
    return pl.pallas_call(
        kernel,
        out_shape=jax.ShapeDtypeStruct((192, TOK), BF16),
        in_specs=[vmem, vmem, vmem, anywhere, anywhere, anywhere],
        out_specs=vmem,
        scratch_shapes=[
            pltpu.VMEM((2, D, HID), BF16),
            pltpu.VMEM((HID, D), BF16),
            pltpu.VMEM((NT, 8 * CAP, 128), BF16),
            pltpu.VMEM((4, 8 * CAP, 512), BF16),
            pltpu.VMEM((8 * CAP, 128), BF16),
            pltpu.VMEM((4, 8, CAP, 512), BF16),
            pltpu.VMEM((NT, CAP, 128), BF16),
            pltpu.VMEM((2, 8 * CAP, HID), F32),
            pltpu.VMEM((8 * CAP, TOK), BF16),
            pltpu.VMEM((8 * CAP, TOK), BF16),
            pltpu.VMEM((HID, HID), BF16),
            pltpu.VMEM((2 * HID, 2 * HID), BF16),
            pltpu.VMEM((8 * CAP, HID), BF16),
            pltpu.VMEM((8 * CAP, HID), BF16),
            pltpu.VMEM((8 * CAP, HID), BF16),
            pltpu.VMEM((8 * CAP, HID), BF16),
            pltpu.VMEM((NT, 8 * CAP, 128), BF16),
            pltpu.VMEM((15872, 128), BF16),
            pltpu.VMEM((4, 8, 4, CAP, 128), BF16),
            pltpu.VMEM((4, 8, 4, CAP, 128), BF16),
            pltpu.VMEM((4, NZ, CAP, 128), BF16),
            pltpu.VMEM((3, NZ, CAP, 128), BF16),
            pltpu.VMEM((NZ - 1, CAP, 128), BF16),
            pltpu.VMEM((8 * CAP, 128), BF16),
            dma((4,)), dma((91,)), dma((2,)), dma((2,)), dma((5,)),
        ],
        compiler_params=pltpu.CompilerParams(
            collective_id=0, has_side_effects=True, vmem_limit_bytes=60 * 2**20
        ),
        cost_estimate=pl.CostEstimate(flops=10**10, bytes_accessed=2 * 10**7, transcendentals=2**18),
        name="moe_layer",
    )(routes.T, gate_num.T, tokens, gate_weight[0], up_weight[0], down_weight[0]).T


def solution(mesh):
    placed = (
        P("expert", None),
        P("expert", None),
        P("expert", None),
        P("expert", None, "tensor"),
        P("expert", None, "tensor"),
        P("expert", "tensor", None),
    )
    return jax.shard_map(
        shards, mesh=mesh, in_specs=placed, out_specs=P("expert", "tensor"), check_vma=False
    )
```
